32 devices in a mesh: seq: 4 (over y, core), fsdp: 8 (over z, x).
Axes of the slice: x: 2, y: 2, z: 4, core: 2. Of those that a mesh axis runs over, the one named last changes fastest.
Arguments:
- tokens: bfloat16 [8, 1536, 768], P('fsdp', 'seq'), may hold values from -6 to 6
- cotangent: bfloat16 [8, 1536, 768], P('fsdp', 'seq'), may hold values from -6 to 6
- expert_ids: int32 [8, 1536, 1], P('fsdp', 'seq'), may hold values from 0 to 7; in each aligned block of 384 rows (0 to 383, 384 to 767, ..., all dimensions but the last counted through in order) at most 64 rows name the same one
- bucket_ids: int32 [3071], replicated, may hold values from 0 to 31
- first_gain: bfloat16 [768], P('fsdp'), may hold values from 0.5 to 1.5
- query_weight: bfloat16 [768, 768], P('fsdp'), may hold values from -0.02734375 to 0.02734375
- key_weight: bfloat16 [768, 768], P('fsdp'), may hold values from -0.21875 to 0.21875
- value_weight: bfloat16 [768, 768], P('fsdp'), may hold values from -0.21875 to 0.21875
- output_weight: bfloat16 [768, 768], P('fsdp'), may hold values from -3 to 3
- bias_table: bfloat16 [12, 32], P('seq'), may hold values from -6 to 6
- second_gain: bfloat16 [768], P('fsdp'), may hold values from 0.5 to 1.5
- router_weight: bfloat16 [768, 8], P('fsdp'), may hold values from -0.15625 to 0.15625
- inner_weight: bfloat16 [8, 768, 3072], P('fsdp'), may hold values from -0.21875 to 0.21875
- outer_weight: bfloat16 [8, 3072, 768], P('fsdp'), may hold values from -0.875 to 0.875
Outputs:
- layer_out: bfloat16 [8, 1536, 768], P('fsdp', 'seq')
- tokens_grad: bfloat16 [8, 1536, 768], P('fsdp', 'seq')
- first_gain_grad: float32 [768], P(('seq', 'fsdp'))
- query_grad: float32 [768, 768], P('fsdp', 'seq')
- key_grad: float32 [768, 768], P('fsdp', 'seq')
- value_grad: float32 [768, 768], P('fsdp', 'seq')
- output_grad: float32 [768, 768], P(('seq', 'fsdp'))
- table_grad: float32 [12, 32], P('seq')
- second_gain_grad: float32 [768], P(('seq', 'fsdp'))
- router_grad: float32 [768, 8], P(('seq', 'fsdp'))
- inner_grad: float32 [8, 768, 3072], P('fsdp', None, 'seq')
- outer_grad: float32 [8, 3072, 768], P('fsdp', 'seq')
The draws below stay inside these ranges and needn't reach their ends.
Inputs may be any that keep to these rules, and one draw needn't show every extreme that they name: `expert_ids`: within one block of 384 consecutive tokens of a sequence no expert is named more than 64 times; some expert reaches 64 in some block.
All inputs are finite; a program needn't handle non-finite values.
Results may differ from the reference program's by a relative error of at most 0.019.
Values may be sent and summed in bfloat16 or wider, within the bound.
No kernel may reach another device: no remote copies, remote signals or barrier semaphores. Data moves between devices by JAX's collectives and lax.ppermute only.
A program may use at most 192 MiB of HBM per device.

```python
import math
import jax
import jax.numpy as jnp
import numpy as np
from jax import lax

D = 768
H = 12
DH = 64
FF = 3072
NB = 32
LENGTH = 1536
EXPERTS = 8
SEQS = 8
TOK_DEV = 384
CAP = 64
N_SEQ = 4


def plant(values, stream_key, low, high):
    extent = values.shape
    index_at = [jax.random.randint(jax.random.fold_in(stream_key, axis), (), 0, extent[axis]) for axis in range(len(extent))]
    values = values.at[tuple(index_at)].set(low)
    longest = extent.index(max(extent))
    index_at[longest] = (index_at[longest] + 1) % extent[longest]
    return values.at[tuple(index_at)].set(high)


def steps_of(own_key, extent, cuts, smallest, largest):
    level = 1.0
    for position, blocks in cuts:
        draws = jax.random.uniform(jax.random.fold_in(jax.random.fold_in(own_key, 6), position), (blocks,), jnp.float32, smallest / len(cuts), largest / len(cuts))
        level = level * jnp.repeat(jnp.exp(draws), extent[position] // blocks).reshape((-1,) + (1,) * (len(extent) - 1 - position))
    return level


def routed_block(stream_key, own, number, rows, number_of, top, reach, lean):
    ranking = jax.random.permutation(stream_key, number_of)
    packed, ordinary = portions_of(number_of, rows * top, reach, lean, True), portions_of(number_of, rows * top, reach, lean, False)
    places = jnp.arange(number_of)

    def named(sizes, offset_by):
        used = int((sizes > 0).sum())
        fixed = max(1, used // 4)
        passed = fixed + (places - fixed + offset_by * (used - fixed)) % max(1, number_of - fixed)
        return jnp.zeros((number_of,), jnp.int32).at[ranking[jnp.where(places < fixed, places, passed)]].set(jnp.asarray(sizes, jnp.int32))

    sizes = jnp.where(number % 4 == 0, named(packed, number // 4), named(ordinary, number - number // 4 - 1))
    mixed = jax.random.permutation(jax.random.fold_in(own, 3), number_of)
    donor, receiver = mixed[0:number_of // 2 * 2:2], mixed[1:number_of // 2 * 2:2]
    room = jnp.minimum(sizes[donor] - 1, reach - sizes[receiver]) // 2
    room = jnp.where((donor == ranking[0]) | (receiver == ranking[0]) | (sizes[receiver] == 0), 0, jnp.maximum(room, 0))
    passed = jax.random.randint(jax.random.fold_in(own, 4), (number_of // 2,), 0, 1 << 20) % (room + 1)
    sizes = sizes.at[donor].add(-passed).at[receiver].add(passed)
    labels = jnp.searchsorted(jnp.cumsum(sizes), jnp.arange(rows * top), side="right").astype(jnp.int32)
    listing = labels.reshape(top, rows).T
    listing = listing[jax.random.permutation(jax.random.fold_in(own, 1), rows)]
    offset_by = jax.random.randint(jax.random.fold_in(own, 2), (rows, 1), 0, top)
    return jnp.take_along_axis(listing, (jnp.arange(top)[None, :] + offset_by) % top, axis=1)


def portions_of(count, total, reach, slope, full):
    loads = [(1 << 20) // math.isqrt(grade ** slope) + 1 for grade in range(1, count + 1)]
    largest = reach if full else min(reach, max(-(-total // count), total * loads[0] // sum(loads)))
    least = 1 if total - largest >= count - 1 else 0
    counts, rest = [largest] + [least] * (count - 1), total - largest - least * (count - 1)
    while rest > 0:
        free = [i for i in range(1, count) if counts[i] < largest] or [i for i in range(1, count) if counts[i] < reach]
        mass, left = sum([loads[i] for i in free]), rest
        for i in free:
            addition = min(reach - counts[i], max(1, left * loads[i] // mass), rest)
            counts[i] = counts[i] + addition
            rest = rest - addition
    return np.array(counts)


def bell_draw(own_key, dims, spread, reach, split=(), kind=jnp.bfloat16):
    entries = jax.random.normal(own_key, dims, jnp.float32) * spread
    if len(split) > 0:
        entries = steps_of(own_key, dims, split, -0.22, 0.18) * entries
    return jnp.clip(entries, min=-reach, max=reach).astype(kind)


def setup_inputs(seed: int = 0) -> dict:
    key_of = jax.random.split(jax.random.key(seed), 15)
    tokens = bell_draw(key_of[0], (SEQS, LENGTH, D), 1.0, 6.0, ((0, 8), (1, 4)))
    cotangent = bell_draw(key_of[1], (SEQS, LENGTH, D), 1.0, 6.0, ((0, 8), (1, 4)))
    expert_ids_keys = jax.random.split(jax.random.fold_in(key_of[2], 1), SEQS * LENGTH // TOK_DEV)
    expert_ids_turns = jax.random.permutation(jax.random.fold_in(key_of[2], 3), SEQS * LENGTH // TOK_DEV)
    expert_ids = jax.vmap(lambda own, number: routed_block(jax.random.fold_in(key_of[2], 2), own, number, TOK_DEV, EXPERTS, 1, CAP, 1))(expert_ids_keys, expert_ids_turns).reshape((SEQS, LENGTH, 1))
    bucket_ids = plant(jax.random.randint(key_of[3], (2 * LENGTH - 1,), 0, NB), jax.random.fold_in(key_of[3], 1), 0, NB - 1).astype(jnp.int32)
    first_gain = jnp.clip(1.0 + 0.1 * jax.random.normal(key_of[4], (D,), jnp.float32), 0.5, 1.5).astype(jnp.bfloat16)
    query_weight = bell_draw(key_of[5], (D, D), (D * DH) ** -0.5, 0.02734375, ((0, 8),))
    key_weight = bell_draw(key_of[6], (D, D), D ** -0.5, 0.21875, ((0, 8),))
    value_weight = bell_draw(key_of[7], (D, D), D ** -0.5, 0.21875, ((0, 8),))
    output_weight = bell_draw(key_of[8], (D, D), (max(1, D // 192)) ** -0.5, 3.0, ((0, 8),))
    bias_table = bell_draw(key_of[9], (H, NB), 1.0, 6.0, ((0, 4),))
    second_gain = jnp.clip(1.0 + 0.1 * jax.random.normal(key_of[10], (D,), jnp.float32), 0.5, 1.5).astype(jnp.bfloat16)
    router_weight = bell_draw(key_of[11], (D, EXPERTS), (2 * D) ** -0.5, 0.15625, ((0, 8),))
    inner_weight = bell_draw(key_of[12], (EXPERTS, D, FF), D ** -0.5, 0.21875, ((0, 8),))
    outer_weight = bell_draw(key_of[13], (EXPERTS, FF, D), (max(1, FF // (EXPERTS * EXPERTS))) ** -0.5, 0.875, ((0, 8),))
    return dict(tokens=tokens, cotangent=cotangent, expert_ids=expert_ids, bucket_ids=bucket_ids, first_gain=first_gain, query_weight=query_weight, key_weight=key_weight, value_weight=value_weight, output_weight=output_weight, bias_table=bias_table, second_gain=second_gain, router_weight=router_weight, inner_weight=inner_weight, outer_weight=outer_weight)


@jax.custom_vjp
def low(v):
    return lax.optimization_barrier(v.astype(jnp.bfloat16)).astype(jnp.float32)

@jax.custom_vjp
def low_back(v):
    return v

def low_keep(v):
    return (low(v), None)

def low_pass(kept, grad):
    return (grad,)

def back_keep(v):
    return (v, None)

def back_low(kept, grad):
    return (low(grad),)
low.defvjp(low_keep, low_pass)
low_back.defvjp(back_keep, back_low)
EPSILON = 1e-06
HIGHEST = lax.Precision.HIGHEST

def rms_norm(values, gain_vector):
    factor = lax.rsqrt(lax.optimization_barrier(jnp.mean(values * values, axis=-1, keepdims=True)) + EPSILON)
    return values * factor * gain_vector

def one_sequence(tokens, params, expert_ids, bucket_ids):
    first_gain, query_weight, key_weight, value_weight, output_weight, bias_table, second_gain, router_weight, inner_weight, outer_weight = params
    length, feature_width = tokens.shape
    head_count = bias_table.shape[0]
    normed = low(rms_norm(tokens, first_gain))
    query_rows = low(low_back(jnp.dot(normed, query_weight, precision=HIGHEST))).reshape(length, head_count, -1)
    key_rows = low(low_back(jnp.dot(normed, key_weight, precision=HIGHEST))).reshape(length, head_count, -1)
    value_rows = low(low_back(jnp.dot(normed, value_weight, precision=HIGHEST))).reshape(length, head_count, -1)
    positions = jnp.arange(length, dtype=jnp.int32)
    offsets = positions[None, :] - positions[:, None] + length - 1
    position_bias = jnp.take(bias_table, bucket_ids[offsets], axis=1)
    scores = low_back(jnp.einsum('ihd,jhd->hij', query_rows, key_rows, precision=HIGHEST) + position_bias)
    attention = low(jax.nn.softmax(scores, axis=-1))
    attended = low(low_back(jnp.einsum('hij,jhd->ihd', attention, value_rows, precision=HIGHEST)))
    attended = attended.reshape(length, feature_width)
    hidden = tokens + low_back(jnp.dot(attended, output_weight, precision=HIGHEST))
    normed_two = low(rms_norm(hidden, second_gain))
    logits = low_back(jnp.dot(normed_two, router_weight, precision=HIGHEST))
    router_probs = jax.nn.softmax(logits, axis=-1)
    expert_count = router_weight.shape[1]
    chosen = expert_ids[:, 0]
    gate_values = jnp.take_along_axis(router_probs, chosen[:, None], axis=1)[:, 0]
    stretch_rows = length // N_SEQ
    hot_choice = (chosen[:, None] == jnp.arange(expert_count, dtype=jnp.int32)[None, :]).astype(jnp.int32)
    hot_blocks = hot_choice.reshape(N_SEQ, stretch_rows, expert_count)
    earlier = jnp.cumsum(hot_blocks, axis=1, dtype=jnp.int32) - hot_blocks
    slot_index = lax.optimization_barrier(jnp.sum(earlier * hot_blocks, axis=2, dtype=jnp.int32)).reshape(length)
    block_index = positions // stretch_rows
    slot_rows = jnp.zeros((expert_count, N_SEQ, CAP, feature_width), jnp.float32)
    slot_rows = slot_rows.at[chosen, block_index, slot_index].set(normed_two)
    slot_rows = low_back(slot_rows).reshape(expert_count, N_SEQ * CAP, feature_width)
    pre_act = low_back(jnp.einsum('esd,edf->esf', slot_rows, inner_weight, precision=HIGHEST))
    active = low(jax.nn.gelu(pre_act))
    expert_out = low(low_back(jnp.einsum('esf,efd->esd', active, outer_weight, precision=HIGHEST)))
    picked = expert_out.reshape(expert_count, N_SEQ, CAP, feature_width)[chosen, block_index, slot_index]
    return hidden + gate_values[:, None] * picked

def reference(tokens, cotangent, expert_ids, bucket_ids, first_gain, query_weight, key_weight, value_weight, output_weight, bias_table, second_gain, router_weight, inner_weight, outer_weight):
    params = tuple((weight_item.astype(jnp.float32) for weight_item in (first_gain, query_weight, key_weight, value_weight, output_weight, bias_table, second_gain, router_weight, inner_weight, outer_weight)))

    def one_step(running, sequence):
        seq_tokens, seq_cotangent, seq_experts = sequence

        def forward(inputs, *weights):
            return one_sequence(inputs, weights, seq_experts, bucket_ids)
        layer_value, pull_back = jax.vjp(forward, seq_tokens.astype(jnp.float32), *params)
        all_grads = pull_back(seq_cotangent.astype(jnp.float32))
        running = tuple((old_sum + new_term for old_sum, new_term in zip(running, all_grads[1:])))
        return (running, (layer_value.astype(jnp.bfloat16), all_grads[0].astype(jnp.bfloat16)))
    initial = tuple((jnp.zeros_like(weight_item) for weight_item in params))
    running, (layer_out, tokens_grad) = lax.scan(one_step, initial, (tokens, cotangent, expert_ids))
    return (layer_out, tokens_grad, running[0], running[1], running[2], running[3], running[4], running[5], running[6], running[7], running[8], running[9])
```

```python
import functools

import jax
import jax.numpy as jnp
from jax import lax
from jax.experimental import pallas as pl
from jax.experimental.pallas import tpu as pltpu
from jax.sharding import PartitionSpec as P

EPSILON = 1e-06


def rms_norm(values, gain_vector):
    factor = lax.rsqrt(jnp.mean(values * values, axis=-1, keepdims=True) + EPSILON)
    return values * factor * gain_vector


def gelu_back(inputs, output_grads):
    _, pull_back = jax.vjp(jax.nn.gelu, inputs)
    return pull_back(output_grads)[0]


STRIP = 128
VMEM_LIMIT = 56 * 1024 * 1024
NT = (((1,), (1,)), ((), ()))
NN = (((1,), (0,)), ((), ()))


def strip_kernel(table_ref, bucket_ref, strip_ref):
    heads = strip_ref.shape[0]
    bucket_count = table_ref.shape[1]
    span = bucket_ref.shape[1]
    ids = lax.broadcasted_iota(jnp.int32, (bucket_count, span), 0)
    hot = jnp.where(ids == bucket_ref[...], 1.0, 0.0).astype(jnp.bfloat16)
    relative = lax.dot_general(table_ref[...], hot, NN, preferred_element_type=jnp.float32)
    for head in range(heads):
        wide = jnp.broadcast_to(relative[head : head + 1, :], (STRIP, span))
        strip_ref[head] = pltpu.roll(wide, span - STRIP + 1, 1, stride=1, stride_axis=0)


def make_strip(table, bucket_row):
    heads, bucket_count = table.shape
    padded = jnp.pad(table, ((0, 16 - heads), (0, 0)))
    span = bucket_row.shape[1]
    return pl.pallas_call(
        strip_kernel,
        out_shape=jax.ShapeDtypeStruct((heads, STRIP, span), jnp.float32),
        compiler_params=pltpu.CompilerParams(vmem_limit_bytes=VMEM_LIMIT),
    )(padded, bucket_row)


def attend_kernel(q_ref, k_ref, v_ref, strip_ref, o_ref, o32_ref, lse_ref, vext_ref, *, heads, size, rows):
    length, width = k_ref.shape
    step = pl.program_id(0)

    @pl.when(step == 0)
    def _():
        vext_ref[:, :width] = v_ref[...]
        vext_ref[:, width:] = jnp.ones((length, 256 - width), jnp.bfloat16)

    for part in range(rows // STRIP):
        block = step * (rows // STRIP) + part
        start = pl.multiple_of((length // STRIP - 1 - block) * STRIP, STRIP)
        q = q_ref[part * STRIP : (part + 1) * STRIP, :]
        owner = lax.broadcasted_iota(jnp.int32, (STRIP, width), 1) // size
        lanes = lax.broadcasted_iota(jnp.int32, (STRIP, 128), 1)
        total = jnp.zeros((STRIP, width), jnp.float32)
        logs = jnp.zeros((STRIP, 128), jnp.float32)
        for head in range(heads):
            qh = jnp.where(owner == head, q, jnp.zeros_like(q))
            s = lax.dot_general(qh, k_ref[...], NT, preferred_element_type=jnp.float32)
            s = s + strip_ref[head, :, pl.ds(start, length)]
            high = jnp.max(s, axis=1, keepdims=True)
            p = jnp.exp(s - high).astype(jnp.bfloat16)
            mixed = lax.dot_general(p, vext_ref[...], NN, preferred_element_type=jnp.float32)
            sums = mixed[:, width : width + 1]
            total = jnp.where(owner == head, mixed[:, :width] * (1.0 / sums), total)
            logs = jnp.where(lanes == head, high + jnp.log(sums), logs)
        sl = slice(part * STRIP, (part + 1) * STRIP)
        o_ref[sl, :] = total.astype(jnp.bfloat16)
        o32_ref[sl, :] = total
        lse_ref[sl, :] = logs


def attend(q, k, v, strip, size, rows=256):
    length, width = q.shape
    heads = width // size
    full = lambda shape: pl.BlockSpec(shape, lambda i: (0,) * len(shape))
    return pl.pallas_call(
        functools.partial(attend_kernel, heads=heads, size=size, rows=rows),
        grid=(length // rows,),
        in_specs=[
            pl.BlockSpec((rows, width), lambda i: (i, 0)),
            full((length, width)),
            full((length, width)),
            full(strip.shape),
        ],
        out_specs=[
            pl.BlockSpec((rows, width), lambda i: (i, 0)),
            pl.BlockSpec((rows, width), lambda i: (i, 0)),
            pl.BlockSpec((rows, 128), lambda i: (i, 0)),
        ],
        out_shape=[
            jax.ShapeDtypeStruct((length, width), jnp.bfloat16),
            jax.ShapeDtypeStruct((length, width), jnp.float32),
            jax.ShapeDtypeStruct((length, 128), jnp.float32),
        ],
        scratch_shapes=[pltpu.VMEM((length, 256), jnp.bfloat16)],
        compiler_params=pltpu.CompilerParams(vmem_limit_bytes=VMEM_LIMIT),
    )(q, k, v, strip)


def three_parts(value):
    first = value.astype(jnp.bfloat16)
    rest = value - first.astype(jnp.float32)
    second = rest.astype(jnp.bfloat16)
    third = (rest - second.astype(jnp.float32)).astype(jnp.bfloat16)
    return first, second, third


def attend_back_kernel(
    q_ref, k_ref, v_ref, o32_ref, do_ref, lse_ref, strip_ref,
    dq_ref, dkt_ref, dvt_ref, strip_grad_ref,
    kext_ref, vext_ref, *, heads, size, rows,
):
    length, width = k_ref.shape
    step = pl.program_id(0)

    @pl.when(step == 0)
    def _():
        ones = jnp.ones((length, 256 - width), jnp.bfloat16)
        kext_ref[:, :width] = k_ref[...]
        kext_ref[:, width:] = ones
        vext_ref[:, :width] = v_ref[...]
        vext_ref[:, width:] = ones
        dkt_ref[...] = jnp.zeros_like(dkt_ref)
        dvt_ref[...] = jnp.zeros_like(dvt_ref)
        strip_grad_ref[...] = jnp.zeros_like(strip_grad_ref)

    for part in range(rows // STRIP):
        block = step * (rows // STRIP) + part
        start = pl.multiple_of((length // STRIP - 1 - block) * STRIP, STRIP)
        sl = slice(part * STRIP, (part + 1) * STRIP)
        q = q_ref[sl, :]
        do = do_ref[sl, :]
        qt = q.astype(jnp.float32).T.astype(jnp.bfloat16)
        dot_ = do.astype(jnp.float32).T.astype(jnp.bfloat16)
        prod = do.astype(jnp.float32) * o32_ref[sl, :]
        owner = lax.broadcasted_iota(jnp.int32, (STRIP, width), 1) // size
        tail = lax.broadcasted_iota(jnp.int32, (STRIP, 256 - width), 1)
        total = jnp.zeros((STRIP, width), jnp.float32)

        def extend(rows_, value):
            first, second, third = three_parts(value)
            ext = jnp.where(tail == 0, first, jnp.where(tail == 1, second, jnp.where(tail == 2, third, jnp.zeros_like(third))))
            return jnp.concatenate([rows_, ext], axis=1)

        for head in range(heads):
            mine = owner == head
            rs = slice(head * size, (head + 1) * size)
            qh = jnp.where(mine, q, jnp.zeros_like(q))
            doh = jnp.where(mine, do, jnp.zeros_like(do))
            delta = jnp.sum(jnp.where(mine, prod, 0.0), axis=1, keepdims=True)
            lse = lse_ref[sl, head : head + 1]
            s = lax.dot_general(extend(qh, -lse), kext_ref[...], NT, preferred_element_type=jnp.float32)
            p = jnp.exp(s + strip_ref[head, :, pl.ds(start, length)])
            dp = lax.dot_general(extend(doh, -delta), vext_ref[...], NT, preferred_element_type=jnp.float32)
            ds = p * dp
            strip_grad_ref[head, :, pl.ds(start, length)] += ds
            ds = ds.astype(jnp.bfloat16)
            p = p.astype(jnp.bfloat16)
            dvt_ref[rs, :] += lax.dot_general(dot_[rs, :], p, NN, preferred_element_type=jnp.float32)
            dkt_ref[rs, :] += lax.dot_general(qt[rs, :], ds, NN, preferred_element_type=jnp.float32)
            dq = lax.dot_general(ds, k_ref[...], NN, preferred_element_type=jnp.float32)
            total = jnp.where(mine, dq, total)
        dq_ref[sl, :] = total.astype(jnp.bfloat16)


def attend_back(q, k, v, o32, do, lse, strip, size, rows=256):
    length, width = q.shape
    heads = width // size
    full = lambda shape: pl.BlockSpec(shape, lambda i: (0,) * len(shape))
    blk = lambda w: pl.BlockSpec((rows, w), lambda i: (i, 0))
    return pl.pallas_call(
        functools.partial(attend_back_kernel, heads=heads, size=size, rows=rows),
        grid=(length // rows,),
        in_specs=[blk(width), full((length, width)), full((length, width)), blk(width), blk(width), blk(128), full(strip.shape)],
        out_specs=[blk(width), full((width, length)), full((width, length)), full(strip.shape)],
        out_shape=[
            jax.ShapeDtypeStruct((length, width), jnp.bfloat16),
            jax.ShapeDtypeStruct((width, length), jnp.float32),
            jax.ShapeDtypeStruct((width, length), jnp.float32),
            jax.ShapeDtypeStruct(strip.shape, jnp.float32),
        ],
        scratch_shapes=[pltpu.VMEM((length, 256), jnp.bfloat16), pltpu.VMEM((length, 256), jnp.bfloat16)],
        compiler_params=pltpu.CompilerParams(vmem_limit_bytes=VMEM_LIMIT),
    )(q, k, v, o32, do, lse, strip)


def table_kernel(strip_grad_ref, bucket_ref, out_ref, *, heads, bucket_count):
    span = strip_grad_ref.shape[2]
    rows = []
    for head in range(heads):
        folded = strip_grad_ref[head]
        half = STRIP // 2
        while half >= 1:
            folded = pltpu.roll(folded[:half], half, 1) + folded[half:]
            half //= 2
        rows.append(folded)
    diag = jnp.concatenate(rows + [jnp.zeros((8 - heads, span), jnp.float32)], axis=0)
    ids = lax.broadcasted_iota(jnp.int32, (bucket_count, span), 0)
    hot = jnp.where(ids == bucket_ref[...], 1.0, 0.0)
    out_ref[...] = lax.dot_general(diag, hot, NT, preferred_element_type=jnp.float32, precision=lax.Precision.HIGHEST)


def table_sum(strip_grad, bucket_row, bucket_count):
    heads = strip_grad.shape[0]
    return pl.pallas_call(
        functools.partial(table_kernel, heads=heads, bucket_count=bucket_count),
        out_shape=jax.ShapeDtypeStruct((8, bucket_count), jnp.float32),
        compiler_params=pltpu.CompilerParams(vmem_limit_bytes=VMEM_LIMIT),
    )(strip_grad, bucket_row)[:heads]


def on_device(
    tokens,
    cotangent,
    expert_ids,
    bucket_ids,
    first_gain,
    query_weight,
    key_weight,
    value_weight,
    output_weight,
    bias_table,
    second_gain,
    router_weight,
    inner_weight,
    outer_weight,
):
    gathered = (
        lax.all_gather(first_gain, "fsdp", axis=0, tiled=True),
        lax.all_gather(query_weight, "fsdp", axis=0, tiled=True),
        lax.all_gather(key_weight, "fsdp", axis=0, tiled=True),
        lax.all_gather(value_weight, "fsdp", axis=0, tiled=True),
        lax.all_gather(output_weight, "fsdp", axis=0, tiled=True),
        lax.all_gather(second_gain, "fsdp", axis=0, tiled=True),
        lax.all_gather(router_weight, "fsdp", axis=0, tiled=True),
    )
    gain_one, full_query, full_key, full_value, full_output, gain_two, full_router = gathered
    gain_one = gain_one.astype(jnp.float32)
    gain_two = gain_two.astype(jnp.float32)
    token_count = tokens.shape[1]
    feature_width = tokens.shape[2]
    expert_count = full_router.shape[1]
    capacity = max(2, 4 * token_count // (3 * expert_count))
    group_count = lax.axis_size("seq")
    width_share = feature_width // group_count
    inputs = tokens[0].astype(jnp.float32)
    normed = rms_norm(inputs, gain_one).astype(jnp.bfloat16)
    query_rows = jnp.dot(normed, full_query, preferred_element_type=jnp.float32).astype(
        jnp.bfloat16
    )
    key_rows = jnp.dot(normed, full_key, preferred_element_type=jnp.float32).astype(jnp.bfloat16)
    value_rows = jnp.dot(normed, full_value, preferred_element_type=jnp.float32).astype(
        jnp.bfloat16
    )
    query_heads, key_heads, value_heads = (
        lax.all_to_all(query_rows, "seq", split_axis=1, concat_axis=0, tiled=True),
        lax.all_to_all(key_rows, "seq", split_axis=1, concat_axis=0, tiled=True),
        lax.all_to_all(value_rows, "seq", split_axis=1, concat_axis=0, tiled=True),
    )
    head_size = width_share // bias_table.shape[0]
    bucket_count = bias_table.shape[1]
    bucket_row = jnp.pad(bucket_ids, (0, 1))[None]
    strip = make_strip(bias_table, bucket_row)
    mixed_rows, mixed_wide, log_totals = attend(
        query_heads, key_heads, value_heads, strip, head_size
    )
    attended = lax.all_to_all(mixed_rows, "seq", split_axis=0, concat_axis=1, tiled=True)
    hidden = inputs + jnp.dot(attended, full_output, preferred_element_type=jnp.float32)
    normed_two = rms_norm(hidden, gain_two).astype(jnp.bfloat16)
    logits = jnp.dot(normed_two, full_router, preferred_element_type=jnp.float32)
    router_probs = jax.nn.softmax(logits, axis=-1)
    chosen = expert_ids[0, :, 0]
    hot_choice = chosen[:, None] == jnp.arange(expert_count, dtype=jnp.int32)[None, :]
    hot_counts = hot_choice.astype(jnp.int32)
    earlier = jnp.cumsum(hot_counts, axis=0, dtype=jnp.int32) - hot_counts
    slot_index = jnp.sum(earlier * hot_counts, axis=1, dtype=jnp.int32)
    placement = chosen * capacity + slot_index
    gate_values = jnp.sum(jnp.where(hot_choice, router_probs, 0.0), axis=1)
    slot_ids = jnp.arange(expert_count * capacity, dtype=jnp.int32)
    dispatch_map = (placement[:, None] == slot_ids[None, :]).astype(jnp.bfloat16)
    sent_slots = jnp.einsum(
        "tm,td->md", dispatch_map, normed_two, preferred_element_type=jnp.float32
    )
    sent_slots = sent_slots.astype(jnp.bfloat16).reshape(expert_count, capacity, feature_width)
    received = lax.all_to_all(sent_slots, "fsdp", split_axis=0, concat_axis=1, tiled=True)
    pre_act = jnp.einsum("esd,edf->esf", received, inner_weight, preferred_element_type=jnp.float32)
    active = jax.nn.gelu(pre_act).astype(jnp.bfloat16)
    expert_out = jnp.einsum(
        "esf,efd->esd", active, outer_weight, preferred_element_type=jnp.float32
    ).astype(jnp.bfloat16)
    returned = lax.all_to_all(expert_out, "fsdp", split_axis=1, concat_axis=0, tiled=True)
    picked = jnp.take(
        returned.reshape(expert_count * capacity, feature_width), placement, axis=0
    ).astype(jnp.float32)
    layer_out = (hidden + gate_values[:, None] * picked).astype(jnp.bfloat16)[None]
    grad_out = cotangent[0].astype(jnp.float32)
    gate_grad = jnp.sum(grad_out * picked, axis=1)
    picked_grad = (gate_values[:, None] * grad_out).astype(jnp.bfloat16)
    slot_grads = jnp.einsum(
        "tm,td->md", dispatch_map, picked_grad, preferred_element_type=jnp.float32
    )
    slot_grads = slot_grads.astype(jnp.bfloat16).reshape(expert_count, capacity, feature_width)
    result_grad = lax.all_to_all(slot_grads, "fsdp", split_axis=0, concat_axis=1, tiled=True)
    active_grad = jnp.einsum(
        "esd,efd->esf", result_grad, outer_weight, preferred_element_type=jnp.float32
    )
    pre_grad = gelu_back(pre_act, active_grad).astype(jnp.bfloat16)
    input_grad = jnp.einsum(
        "esf,edf->esd", pre_grad, inner_weight, preferred_element_type=jnp.float32
    ).astype(jnp.bfloat16)
    inner_term = jnp.einsum("esd,esf->edf", received, pre_grad, preferred_element_type=jnp.float32)
    outer_term = jnp.einsum("esf,esd->efd", active, result_grad, preferred_element_type=jnp.float32)
    inner_grad, outer_grad = (
        lax.psum_scatter(
            inner_term.astype(jnp.bfloat16), "seq", scatter_dimension=2, tiled=True
        ).astype(jnp.float32),
        lax.psum_scatter(
            outer_term.astype(jnp.bfloat16), "seq", scatter_dimension=1, tiled=True
        ).astype(jnp.float32),
    )
    token_grads = lax.all_to_all(input_grad, "fsdp", split_axis=1, concat_axis=0, tiled=True)
    normed_two_grad = jnp.take(
        token_grads.reshape(expert_count * capacity, feature_width), placement, axis=0
    ).astype(jnp.float32)
    prob_grad = jnp.where(hot_choice, gate_grad[:, None], 0.0)
    logit_grad = (router_probs * (prob_grad - (gate_values * gate_grad)[:, None])).astype(
        jnp.bfloat16
    )
    router_grad = jnp.dot(normed_two.T, logit_grad, preferred_element_type=jnp.float32)
    normed_two_grad = normed_two_grad + jnp.dot(
        logit_grad, full_router.T, preferred_element_type=jnp.float32
    )
    _, second_pull = jax.vjp(rms_norm, hidden, gain_two)
    hidden_part, second_gain_grad = second_pull(normed_two_grad)
    hidden_grad = grad_out + hidden_part
    branch_grad = hidden_grad.astype(jnp.bfloat16)
    output_grad = jnp.dot(attended.T, branch_grad, preferred_element_type=jnp.float32)
    attended_grad = jnp.dot(branch_grad, full_output.T, preferred_element_type=jnp.float32).astype(
        jnp.bfloat16
    )
    mixed_grad = lax.all_to_all(attended_grad, "seq", split_axis=1, concat_axis=0, tiled=True)
    query_back, key_back, value_back, strip_grad = attend_back(
        query_heads, key_heads, value_heads, mixed_wide, mixed_grad, log_totals, strip, head_size
    )
    key_back = key_back.T.astype(jnp.bfloat16)
    value_back = value_back.T.astype(jnp.bfloat16)
    query_rows_grad, key_rows_grad, value_rows_grad = (
        lax.all_to_all(query_back, "seq", split_axis=0, concat_axis=1, tiled=True),
        lax.all_to_all(key_back, "seq", split_axis=0, concat_axis=1, tiled=True),
        lax.all_to_all(value_back, "seq", split_axis=0, concat_axis=1, tiled=True),
    )

    def grouped_term(rows_grad):
        grouped = rows_grad.reshape(token_count, group_count, width_share)
        term = jnp.einsum("td,tsc->sdc", normed, grouped, preferred_element_type=jnp.float32)
        return term.reshape(group_count * feature_width, width_share)

    query_grad, key_grad, value_grad = (
        lax.psum_scatter(
            grouped_term(query_rows_grad), ("seq", "fsdp"), scatter_dimension=0, tiled=True
        ),
        lax.psum_scatter(
            grouped_term(key_rows_grad), ("seq", "fsdp"), scatter_dimension=0, tiled=True
        ),
        lax.psum_scatter(
            grouped_term(value_rows_grad), ("seq", "fsdp"), scatter_dimension=0, tiled=True
        ),
    )
    normed_grad = jnp.dot(query_rows_grad, full_query.T, preferred_element_type=jnp.float32)
    normed_grad = normed_grad + jnp.dot(
        key_rows_grad, full_key.T, preferred_element_type=jnp.float32
    )
    normed_grad = normed_grad + jnp.dot(
        value_rows_grad, full_value.T, preferred_element_type=jnp.float32
    )
    _, first_pull = jax.vjp(rms_norm, inputs, gain_one)
    input_part, first_gain_grad = first_pull(normed_grad)
    tokens_grad = (hidden_grad + input_part).astype(jnp.bfloat16)[None]
    table_local = table_sum(strip_grad, bucket_row, bucket_count)
    table_grad = lax.psum(table_local, "fsdp")
    summed = (
        lax.psum_scatter(first_gain_grad, ("seq", "fsdp"), scatter_dimension=0, tiled=True),
        lax.psum_scatter(output_grad, ("seq", "fsdp"), scatter_dimension=0, tiled=True),
        lax.psum_scatter(second_gain_grad, ("seq", "fsdp"), scatter_dimension=0, tiled=True),
        lax.psum_scatter(router_grad, ("seq", "fsdp"), scatter_dimension=0, tiled=True),
    )
    return (
        layer_out,
        tokens_grad,
        summed[0],
        query_grad,
        key_grad,
        value_grad,
        summed[1],
        table_grad,
        summed[2],
        summed[3],
        inner_grad,
        outer_grad,
    )


def solution(mesh):
    return jax.shard_map(
        on_device,
        mesh=mesh,
        in_specs=(
            P("fsdp", "seq", None),
            P("fsdp", "seq", None),
            P("fsdp", "seq", None),
            P(),
            P("fsdp"),
            P("fsdp", None),
            P("fsdp", None),
            P("fsdp", None),
            P("fsdp", None),
            P("seq", None),
            P("fsdp"),
            P("fsdp", None),
            P("fsdp", None, None),
            P("fsdp", None, None),
        ),
        out_specs=(
            P("fsdp", "seq", None),
            P("fsdp", "seq", None),
            P(("seq", "fsdp")),
            P("fsdp", "seq"),
            P("fsdp", "seq"),
            P("fsdp", "seq"),
            P(("seq", "fsdp"), None),
            P("seq", None),
            P(("seq", "fsdp")),
            P(("seq", "fsdp"), None),
            P("fsdp", None, "seq"),
            P("fsdp", "seq", None),
        ),
        check_vma=False,
    )
```

```python
import functools

import jax
import jax.numpy as jnp
from jax import lax
from jax.experimental import pallas as pl
from jax.experimental.pallas import tpu as pltpu
from jax.sharding import PartitionSpec as P

EPSILON = 1e-06
STRIP = 128
EXTRA = 8
VMEM_LIMIT = 56 * 1024 * 1024
NT = (((1,), (1,)), ((), ()))
NN = (((1,), (0,)), ((), ()))
LOW = jnp.bfloat16
WIDE = jnp.float32


def product(left, right, dims=NN):
    return lax.dot_general(left, right, dims, preferred_element_type=WIDE)


def flip(values):
    return values.astype(WIDE).T.astype(LOW)


def swap(values, axis, offset):
    count = lax.axis_size(axis)
    return lax.ppermute(values, axis, [(i, i ^ offset) for i in range(count)])


def cost(microseconds):
    return pl.CostEstimate(
        flops=int(microseconds * 1.15e9), bytes_accessed=1024, transcendentals=0
    )


def call(kernel, inputs, outputs, scratch=(), where=None, time=2):
    specs = [pl.BlockSpec(memory_space=pltpu.VMEM)] * len(inputs)
    operands = list(inputs)
    if where is not None:
        specs = [pl.BlockSpec(memory_space=pltpu.SMEM)] + specs
        operands = [where] + operands
    return pl.pallas_call(
        kernel,
        in_specs=specs,
        out_specs=[pl.BlockSpec(memory_space=pltpu.VMEM)] * len(outputs),
        out_shape=[jax.ShapeDtypeStruct(shape, dtype) for shape, dtype in outputs],
        scratch_shapes=list(scratch),
        compiler_params=pltpu.CompilerParams(vmem_limit_bytes=VMEM_LIMIT),
        cost_estimate=cost(time),
    )(*operands)


def strip_kernel(table_ref, bucket_ref, strip_ref):
    heads = strip_ref.shape[0]
    span = bucket_ref.shape[1]
    ids = lax.broadcasted_iota(jnp.int32, (table_ref.shape[1], span), 0)
    hot = jnp.where(ids == bucket_ref[...], 1.0, 0.0).astype(LOW)
    relative = product(table_ref[...], hot)
    for head in range(heads):
        wide = jnp.broadcast_to(relative[head : head + 1, :], (STRIP, span))
        strip_ref[head] = pltpu.roll(wide, span - STRIP + 1, 1, stride=1, stride_axis=0)


def forward_kernel(where_ref, *refs, heads, size, seq_count, weight_parts):
    token_refs = refs[:seq_count]
    weight_refs = refs[seq_count : seq_count + weight_parts]
    strip_ref = refs[seq_count + weight_parts]
    (
        normed_ref, q_ref, k_ref, v_ref, wq_ref, wk_ref, wv_ref, extra_ref, o32_ref, share_ref,
        weights_ref,
    ) = refs[seq_count + weight_parts + 1 : seq_count + weight_parts + 12]
    mixed_refs = refs[seq_count + weight_parts + 12 : -2]
    joined_ref, vext_ref = refs[-2:]
    length, width = k_ref.shape
    rows = length // seq_count
    step = pl.program_id(0)
    me = where_ref[0]
    owner_row = where_ref[1]

    @pl.when(step == 0)
    def _():
        if weight_parts == 1:
            joined_ref[...] = weight_refs[0][...]
        else:
            share = weight_refs[0].shape[0]
            offsets = [2 * part for part in range(weight_parts - 2)] + [1]
            for part, offset in enumerate(offsets):
                place = pl.multiple_of((owner_row ^ offset) * share, 16)
                joined_ref[pl.ds(place, share), :] = weight_refs[part][...]
            for part in range(1, weight_parts - 2):
                place = pl.multiple_of((owner_row ^ (2 * part + 1)) * share, 16)
                joined_ref[pl.ds(place, share), :] = weight_refs[-1][
                    (part - 1) * share : part * share, :
                ]
        extra_ref[...] = joined_ref[:, :128].astype(WIDE).T
        joined = joined_ref[...]
        wq_ref[...] = joined[:, 128 : 128 + width]
        wk_ref[...] = joined[:, 128 + width : 128 + 2 * width]
        wv_ref[...] = joined[:, 128 + 2 * width : 128 + 3 * width]
        gain = extra_ref[0:1, :]
        for part in range(seq_count):
            place = pl.ds(pl.multiple_of((me ^ part) * rows, rows), rows)
            inputs = token_refs[part][...].astype(WIDE)
            factor = lax.rsqrt(jnp.mean(inputs * inputs, axis=1, keepdims=True) + EPSILON)
            normed = (inputs * factor * gain).astype(LOW)
            normed_ref[place, :] = normed
            q_ref[place, :] = product(normed, wq_ref[...]).astype(LOW)
            k_ref[place, :] = product(normed, wk_ref[...]).astype(LOW)
            values = product(normed, wv_ref[...]).astype(LOW)
            v_ref[place, :] = values
            vext_ref[place, :width] = values
        vext_ref[:, width:] = jnp.ones((length, 256 - width), LOW)

    for part in range(rows // STRIP):
        block = (me ^ step) * (rows // STRIP) + part
        start = pl.multiple_of((length // STRIP - 1 - block) * STRIP, STRIP)
        q = q_ref[pl.ds(pl.multiple_of(block * STRIP, STRIP), STRIP), :]
        owner = lax.broadcasted_iota(jnp.int32, (STRIP, width), 1) // size
        lanes = lax.broadcasted_iota(jnp.int32, (STRIP, 128), 1)
        total = jnp.zeros((STRIP, width), WIDE)
        shares = jnp.zeros((STRIP, 128), WIDE)
        place = slice(part * STRIP, (part + 1) * STRIP)
        for head in range(heads):
            scores = product(jnp.where(owner == head, q, jnp.zeros_like(q)), k_ref[...], NT)
            scores = scores + strip_ref[head, :, pl.ds(start, length)]
            high = jnp.max(scores, axis=1, keepdims=True)
            weights = jnp.exp(scores - high).astype(LOW)
            mixed = product(weights, vext_ref[...])
            weights_ref[head, place, :] = weights
            share = 1.0 / mixed[:, width : width + 1]
            total = jnp.where(owner == head, mixed[:, :width] * share, total)
            shares = jnp.where(lanes == head, share, shares)
        o32_ref[place, :] = total
        share_ref[place, :] = shares
        for offset in range(seq_count):

            @pl.when(step == offset)
            def _():
                mixed_refs[offset][place, :] = total.astype(LOW)


def forward_attention(where, token_parts, weight_parts, strip, size):
    seq_count = len(token_parts)
    rows, features = token_parts[0].shape
    length = rows * seq_count
    columns = weight_parts[0].shape[1]
    width = (columns - 128) // 3
    heads = width // size
    full = lambda *shape: pl.BlockSpec(shape, lambda i, w: (0,) * len(shape))
    block = lambda w: pl.BlockSpec((rows, w), lambda i, w_: (i, 0))
    shaped = jax.ShapeDtypeStruct
    results = pl.pallas_call(
        functools.partial(
            forward_kernel,
            heads=heads,
            size=size,
            seq_count=seq_count,
            weight_parts=len(weight_parts),
        ),
        grid_spec=pltpu.PrefetchScalarGridSpec(
            num_scalar_prefetch=1,
            grid=(seq_count,),
            in_specs=[full(*a.shape) for a in (*token_parts, *weight_parts, strip)],
            out_specs=[full(length, features)]
            + [full(length, width)] * 3
            + [full(features, width)] * 3
            + [full(128, features), block(width), block(128)]
            + [pl.BlockSpec((heads, rows, length), lambda i, w: (0, i, 0))]
            + [full(rows, width)] * seq_count,
            scratch_shapes=[pltpu.VMEM((features, columns), LOW), pltpu.VMEM((length, 256), LOW)],
        ),
        out_shape=[shaped((length, features), LOW)]
        + [shaped((length, width), LOW)] * 3
        + [shaped((features, width), LOW)] * 3
        + [
            shaped((128, features), WIDE),
            shaped((length, width), WIDE),
            shaped((length, 128), WIDE),
            shaped((heads, length, length), LOW),
        ]
        + [shaped((rows, width), LOW)] * seq_count,
        compiler_params=pltpu.CompilerParams(vmem_limit_bytes=VMEM_LIMIT),
        cost_estimate=cost(35),
    )(where, *token_parts, *weight_parts, strip)
    return results[:11], results[11:]


def place_rows(where_ref, joined_ref, part_refs):
    part_rows = joined_ref.shape[0] // len(part_refs)
    for part, part_ref in enumerate(part_refs):
        place = pl.multiple_of((where_ref[1] ^ part) * part_rows, 16) if len(part_refs) > 1 else 0
        joined_ref[pl.ds(place, part_rows), :] = part_ref[...]


def send_kernel(where_ref, *refs, seq_count, weight_parts, experts, capacity):
    mixed_refs = refs[:seq_count]
    weight_refs = refs[seq_count : seq_count + weight_parts]
    tokens_ref, cotangent_ref, ids_ref, extra_ref = refs[
        seq_count + weight_parts : seq_count + weight_parts + 4
    ]
    rest = refs[seq_count + weight_parts + 4 :]
    hidden_ref, normed_ref, notes_ref = rest[:3]
    both_ref, joined_ref = rest[3:]
    rows = tokens_ref.shape[0]
    width = mixed_refs[0].shape[1]
    place_rows(where_ref, joined_ref, weight_refs)
    hidden = tokens_ref[...].astype(WIDE)
    for part in range(seq_count):
        place = pl.multiple_of((where_ref[0] ^ part) * width, 64)
        hidden = hidden + product(mixed_refs[part][...], joined_ref[pl.ds(place, width), :])
    hidden_ref[...] = hidden
    factor = lax.rsqrt(jnp.mean(hidden * hidden, axis=1, keepdims=True) + EPSILON)
    normed = (hidden * factor * extra_ref[1:2, :]).astype(LOW)
    normed_ref[...] = normed
    logits = product(normed, extra_ref[...].astype(LOW), NT)
    lanes = lax.broadcasted_iota(jnp.int32, (rows, 128), 1)
    valid = (lanes >= EXTRA) & (lanes < EXTRA + experts)
    logits = jnp.where(valid, logits, -jnp.inf)
    powers = jnp.exp(logits - jnp.max(logits, axis=1, keepdims=True))
    probs = powers / jnp.sum(powers, axis=1, keepdims=True)
    ids = ids_ref[...]
    hot = lanes == ids + EXTRA
    gate = jnp.sum(jnp.where(hot, probs, 0.0), axis=1, keepdims=True)
    earlier_rows = lax.broadcasted_iota(jnp.int32, (rows, rows), 1) < lax.broadcasted_iota(
        jnp.int32, (rows, rows), 0
    )
    earlier = product(
        jnp.where(earlier_rows, 1.0, 0.0).astype(LOW), jnp.where(hot, 1.0, 0.0).astype(LOW)
    )
    slot = jnp.sum(jnp.where(hot, earlier, 0.0), axis=1, keepdims=True)
    placement = (ids * (2 * capacity)).astype(WIDE) + slot
    notes = jnp.where(lanes == 0, gate, probs)
    notes = jnp.where(lanes == 1, placement, notes)
    notes = jnp.where(lanes == 2, factor, notes)
    notes = jnp.where(lanes == 3, (ids + EXTRA).astype(WIDE), notes)
    notes_ref[...] = notes
    placement_row = notes.T[1:2, :].astype(jnp.int32)
    slot_ids = lax.broadcasted_iota(jnp.int32, (2 * experts * capacity, rows), 0)
    spread = jnp.concatenate(
        [
            jnp.where(slot_ids == placement_row, 1.0, 0.0).astype(LOW),
            jnp.where(slot_ids == placement_row + capacity, 1.0, 0.0).astype(LOW),
        ],
        axis=1,
    )
    picked_grad = (gate * cotangent_ref[...].astype(WIDE)).astype(LOW)
    both_ref[...] = product(spread, jnp.concatenate([normed, picked_grad], axis=0)).astype(LOW)


def expert_kernel(
    both_ref, inner_ref, outer_ref, active_ref, pre_grad_ref, slots_ref, grads_ref, back_ref,
    out_ref, slots_grad_ref, *, sources,
):
    step = pl.program_id(0)
    slot_count, features = slots_ref.shape
    apart = (sources, 2, slot_count // sources, features)

    @pl.when(step == 0)
    def _():
        both = both_ref[...].astype(WIDE).reshape(apart)
        slots_ref[...] = both[:, 0].reshape(slot_count, features).astype(LOW)
        grads_ref[...] = both[:, 1].reshape(slot_count, features).astype(LOW)
        out_ref[...] = jnp.zeros_like(out_ref)
        slots_grad_ref[...] = jnp.zeros_like(slots_grad_ref)

    pre = product(slots_ref[...], inner_ref[...])
    active_grad = product(grads_ref[...], outer_ref[...], NT)
    scale = 0.7978845608028654
    square = pre * pre
    bent = jnp.tanh(pre * (scale + scale * 0.044715 * square))
    half = 0.5 + 0.5 * bent
    active = (pre * half).astype(LOW)
    slope = half + 0.5 * pre * (1.0 - bent * bent) * (scale + 3.0 * scale * 0.044715 * square)
    pre_grad = (active_grad * slope).astype(LOW)
    active_ref[...] = active
    pre_grad_ref[...] = pre_grad
    out_ref[...] += product(active, outer_ref[...])
    slots_grad_ref[...] += product(pre_grad, inner_ref[...], NT)

    @pl.when(step == pl.num_programs(0) - 1)
    def _():
        each = (sources, 1, slot_count // sources, features)
        back = jnp.concatenate(
            [out_ref[...].reshape(each), slots_grad_ref[...].reshape(each)], axis=1
        )
        back_ref[...] = back.reshape(2 * slot_count, features).astype(LOW)


def expert_step(both, inner, outer, sources, chunk=512):
    slot_count = both.shape[0] // 2
    features, units = inner.shape
    full = lambda *shape: pl.BlockSpec(shape, lambda i: (0,) * len(shape))
    across = pl.BlockSpec((slot_count, chunk), lambda i: (0, i))
    shaped = jax.ShapeDtypeStruct
    return pl.pallas_call(
        functools.partial(expert_kernel, sources=sources),
        grid=(units // chunk,),
        in_specs=[
            full(2 * slot_count, features),
            pl.BlockSpec((features, chunk), lambda i: (0, i)),
            pl.BlockSpec((chunk, features), lambda i: (i, 0)),
        ],
        out_specs=[
            across,
            across,
            full(slot_count, features),
            full(slot_count, features),
            full(2 * slot_count, features),
        ],
        out_shape=[
            shaped((slot_count, units), LOW),
            shaped((slot_count, units), LOW),
            shaped((slot_count, features), LOW),
            shaped((slot_count, features), LOW),
            shaped((2 * slot_count, features), LOW),
        ],
        scratch_shapes=[
            pltpu.VMEM((slot_count, features), WIDE),
            pltpu.VMEM((slot_count, features), WIDE),
        ],
        compiler_params=pltpu.CompilerParams(vmem_limit_bytes=VMEM_LIMIT),
        cost_estimate=cost(24),
    )(both, inner, outer)


def return_kernel(where_ref, *refs, seq_count, weight_parts, experts, capacity):
    mixed_refs = refs[:seq_count]
    weight_refs = refs[seq_count : seq_count + weight_parts]
    refs = refs[seq_count + weight_parts :]
    back_ref = refs[0]
    refs = refs[1:]
    hidden_ref, normed_ref, notes_ref, cotangent_ref, extra_ref = refs[:5]
    layer_ref, hidden_grad_ref, output_grad_ref = refs[5:8]
    mixed_grad_refs = refs[8 : 8 + seq_count]
    joined_ref = refs[-1]
    rows, features = hidden_ref.shape
    width = mixed_refs[0].shape[1]
    place_rows(where_ref, joined_ref, weight_refs)
    notes = notes_ref[...]
    gate = notes[:, 0:1]
    placement = notes[:, 1:2].astype(jnp.int32)
    factor = notes[:, 2:3]
    own_lane = notes[:, 3:4].astype(jnp.int32)
    hidden = hidden_ref[...]
    cotangent = cotangent_ref[...].astype(WIDE)
    slot_ids = lax.broadcasted_iota(jnp.int32, (rows, back_ref.shape[0]), 1)
    picked = product(jnp.where(slot_ids == placement, 1.0, 0.0).astype(LOW), back_ref[...])
    layer_ref[...] = (hidden + gate * picked).astype(LOW)
    gate_grad = jnp.sum(cotangent * picked, axis=1, keepdims=True)
    lanes = lax.broadcasted_iota(jnp.int32, (rows, 128), 1)
    valid = (lanes >= EXTRA) & (lanes < EXTRA + experts)
    probs = jnp.where(valid, notes, 0.0)
    prob_grad = jnp.where(lanes == own_lane, gate_grad, 0.0)
    logit_grad = probs * (prob_grad - gate * gate_grad)
    logit_grad_low = logit_grad.astype(LOW)
    normed_grad = product(
        jnp.where(slot_ids == placement + capacity, 1.0, 0.0).astype(LOW), back_ref[...]
    )
    normed_grad = normed_grad + product(logit_grad_low, extra_ref[...].astype(LOW))
    scaled = normed_grad * hidden
    gain = extra_ref[1:2, :]
    center = jnp.mean(scaled * gain, axis=1, keepdims=True)
    hidden_grad = cotangent + factor * (gain * normed_grad) - hidden * (
        factor * factor * factor * center
    )
    hidden_grad_ref[...] = hidden_grad
    small = product(logit_grad.T.astype(LOW), normed_ref[...])
    gain_grad = jnp.sum(scaled * factor, axis=0, keepdims=True)
    small = jnp.where(lax.broadcasted_iota(jnp.int32, small.shape, 0) == 1, gain_grad, small)
    output_grad_ref[:, features:] = small.T.astype(LOW)
    branch = hidden_grad.astype(LOW)
    for part in range(seq_count):
        place = pl.ds(pl.multiple_of((where_ref[0] ^ part) * width, 64), width)
        mixed_grad_refs[part][...] = product(branch, joined_ref[place, :], NT).astype(LOW)
        output_grad_ref[place, :features] = product(flip(mixed_refs[part][...]), branch).astype(
            LOW
        )


def three_parts(value):
    first = value.astype(LOW)
    rest = value - first.astype(WIDE)
    second = rest.astype(LOW)
    third = (rest - second.astype(WIDE)).astype(LOW)
    return first, second, third


def attend_back_kernel(where_ref, *refs, heads, size, seq_count):
    grad_refs = refs[:seq_count]
    q_ref, k_ref, v_ref, o32_ref, share_ref, weights_ref = refs[seq_count : seq_count + 6]
    dq_ref, dkt_ref, dvt_ref, strip_grad_ref = refs[seq_count + 6 : seq_count + 10]
    vext_ref, grad_ref = refs[seq_count + 10 :]
    length, width = k_ref.shape
    rows = length // seq_count
    step = pl.program_id(0)
    me = where_ref[0]

    @pl.when(step == 0)
    def _():
        vext_ref[:, :width] = v_ref[...]
        vext_ref[:, width:] = jnp.ones((length, 256 - width), LOW)
        dkt_ref[...] = jnp.zeros_like(dkt_ref)
        dvt_ref[...] = jnp.zeros_like(dvt_ref)
        strip_grad_ref[...] = jnp.zeros_like(strip_grad_ref)

    for offset in range(seq_count):

        @pl.when(step == offset)
        def _():
            grad_ref[...] = grad_refs[offset][...]

    for part in range(rows // STRIP):
        block = (me ^ step) * (rows // STRIP) + part
        start = pl.multiple_of((length // STRIP - 1 - block) * STRIP, STRIP)
        token_rows = pl.ds(pl.multiple_of(block * STRIP, STRIP), STRIP)
        own_rows = slice(part * STRIP, (part + 1) * STRIP)
        owner = lax.broadcasted_iota(jnp.int32, (STRIP, width), 1) // size
        tail = lax.broadcasted_iota(jnp.int32, (STRIP, 256 - width), 1)
        share = jnp.zeros((STRIP, width), WIDE)
        for head in range(heads):
            share = jnp.where(owner == head, share_ref[own_rows, head : head + 1], share)
        scaled = grad_ref[own_rows, :].astype(WIDE) * share
        mixed_product = scaled * o32_ref[own_rows, :]
        grad_flipped = scaled.T.astype(LOW)
        scaled = scaled.astype(LOW)
        q_flipped = flip(q_ref[token_rows, :])
        total = jnp.zeros((STRIP, width), WIDE)
        for head in range(heads):
            mine = owner == head
            head_rows = slice(head * size, (head + 1) * size)
            delta = jnp.sum(jnp.where(mine, mixed_product, 0.0), axis=1, keepdims=True)
            first, second, third = three_parts(-delta)
            added = jnp.where(tail == 2, third, jnp.zeros_like(third))
            added = jnp.where(tail == 0, first, jnp.where(tail == 1, second, added))
            own_grad = jnp.concatenate([jnp.where(mine, scaled, jnp.zeros_like(scaled)), added], 1)
            weights = weights_ref[head, own_rows, :]
            score_grad = weights.astype(WIDE) * product(own_grad, vext_ref[...], NT)
            strip_grad_ref[head, :, pl.ds(start, length)] += score_grad
            score_grad = score_grad.astype(LOW)
            dvt_ref[head_rows, :] += product(grad_flipped[head_rows, :], weights)
            dkt_ref[head_rows, :] += product(q_flipped[head_rows, :], score_grad)
            total = jnp.where(mine, product(score_grad, k_ref[...]), total)
        dq_ref[token_rows, :] = total.astype(LOW)


def backward_attention(where, grad_parts, q, k, v, o32, shares, attention, strip_shape):
    seq_count = len(grad_parts)
    length, width = q.shape
    rows = length // seq_count
    heads = attention.shape[0]
    full = lambda *shape: pl.BlockSpec(shape, lambda i, w: (0,) * len(shape))
    block = lambda w: pl.BlockSpec((rows, w), lambda i, w_: (i, 0))
    shaped = jax.ShapeDtypeStruct
    return pl.pallas_call(
        functools.partial(
            attend_back_kernel, heads=heads, size=width // heads, seq_count=seq_count
        ),
        grid_spec=pltpu.PrefetchScalarGridSpec(
            num_scalar_prefetch=1,
            grid=(seq_count,),
            in_specs=[full(rows, width)] * seq_count
            + [full(length, width)] * 3
            + [block(width), block(128)]
            + [pl.BlockSpec((heads, rows, length), lambda i, w: (0, i, 0))],
            out_specs=[
                full(length, width),
                full(width, length),
                full(width, length),
                full(*strip_shape),
            ],
            scratch_shapes=[pltpu.VMEM((length, 256), LOW), pltpu.VMEM((rows, width), LOW)],
        ),
        out_shape=[
            shaped((length, width), LOW),
            shaped((width, length), WIDE),
            shaped((width, length), WIDE),
            shaped(strip_shape, WIDE),
        ],
        compiler_params=pltpu.CompilerParams(vmem_limit_bytes=VMEM_LIMIT),
        cost_estimate=cost(32),
    )(where, *grad_parts, q, k, v, o32, shares, attention)


def weight_kernel(normed_ref, dq_ref, dkt_ref, dvt_ref, out_ref):
    flipped = jnp.concatenate(
        [flip(dq_ref[...]), dkt_ref[...].astype(LOW), dvt_ref[...].astype(LOW)], axis=0
    )
    out_ref[...] = product(flipped, normed_ref[...]).T.astype(LOW)


def row_kernel(
    where_ref, normed_ref, dq_ref, dkt_ref, dvt_ref, wq_ref, wk_ref, wv_ref, extra_ref, *refs,
    seq_count,
):
    row_refs = refs[:seq_count]
    gain_ref, dk_ref, dv_ref = refs[seq_count:]
    length, width = dq_ref.shape
    rows = length // seq_count
    dk_ref[...] = dkt_ref[...].T.astype(LOW)
    dv_ref[...] = dvt_ref[...].T.astype(LOW)
    gain_sum = jnp.zeros((1, normed_ref.shape[1]), WIDE)
    for part in range(seq_count):
        place = pl.ds(pl.multiple_of((where_ref[0] ^ part) * rows, rows), rows)
        row_grad = product(dq_ref[place, :], wq_ref[...], NT)
        row_grad = row_grad + product(dk_ref[place, :], wk_ref[...], NT)
        row_grad = row_grad + product(dv_ref[place, :], wv_ref[...], NT)
        row_refs[part][...] = row_grad.astype(LOW)
        gain_sum = gain_sum + jnp.sum(
            row_grad * normed_ref[place, :].astype(WIDE), axis=0, keepdims=True
        )
    gain_ref[...] = gain_sum / extra_ref[0:1, :]


def table_kernel(strip_grad_ref, bucket_ref, out_ref, *, bucket_count):
    heads, _, span = strip_grad_ref.shape
    sums = []
    for head in range(heads):
        folded = strip_grad_ref[head]
        half = STRIP // 2
        while half >= 1:
            folded = pltpu.roll(folded[:half], half, 1) + folded[half:]
            half //= 2
        sums.append(folded)
    diagonals = jnp.concatenate(sums + [jnp.zeros((8 - heads, span), WIDE)], axis=0)
    ids = lax.broadcasted_iota(jnp.int32, (bucket_count, span), 0)
    hot = jnp.where(ids == bucket_ref[...], 1.0, 0.0)
    out_ref[...] = lax.dot_general(
        diagonals, hot, NT, preferred_element_type=WIDE, precision=lax.Precision.HIGHEST
    )


def finish_kernel(*refs, seq_count):
    row_refs = refs[:seq_count]
    tokens_ref, hidden_grad_ref, extra_ref, out_ref = refs[seq_count:]
    normed_grad = row_refs[0][...].astype(WIDE)
    for part in range(1, seq_count):
        normed_grad = normed_grad + row_refs[part][...].astype(WIDE)
    inputs = tokens_ref[...].astype(WIDE)
    factor = lax.rsqrt(jnp.mean(inputs * inputs, axis=1, keepdims=True) + EPSILON)
    scaled = normed_grad * extra_ref[0:1, :]
    center = jnp.mean(scaled * inputs, axis=1, keepdims=True)
    out_ref[...] = (
        hidden_grad_ref[...] + factor * scaled - inputs * (factor * factor * factor * center)
    ).astype(LOW)


def sum_kernel(parts_ref, *out_refs):
    total = parts_ref[0].astype(WIDE)
    for part in range(1, parts_ref.shape[0]):
        total = total + parts_ref[part].astype(WIDE)
    start = 0
    for out_ref in out_refs:
        width = out_ref.shape[1]
        out_ref[...] = total[:, start : start + width]
        start += width


def on_device(
    tokens,
    cotangent,
    expert_ids,
    bucket_ids,
    first_gain,
    query_weight,
    key_weight,
    value_weight,
    output_weight,
    bias_table,
    second_gain,
    router_weight,
    inner_weight,
    outer_weight,
):
    seq_count = lax.axis_size("seq")
    owner_count = lax.axis_size("fsdp")
    pairwise = owner_count <= 8
    me = lax.axis_index("seq").astype(jnp.int32)
    owner = lax.axis_index("fsdp").astype(jnp.int32)
    rows, features = tokens.shape[1:]
    experts = router_weight.shape[1]
    capacity = max(2, 4 * rows // (3 * experts))
    slot_count = experts * capacity
    heads, bucket_count = bias_table.shape
    width = features // seq_count
    size = width // heads
    where = jnp.stack([me, owner, jnp.zeros_like(owner)])
    weight_parts = owner_count if pairwise else 1

    def exchange(values):
        split = values.reshape(owner_count, -1, values.shape[1])
        return lax.all_to_all(split, "fsdp", 0, 0, tiled=True)

    def exchange_seq(parts):
        return [parts[0]] + [swap(parts[s], "seq", s) for s in range(1, seq_count)]

    token_block = tokens[0]
    grad_block = cotangent[0]
    columns = lambda weight: lax.dynamic_slice_in_dim(weight, me * width, width, 1)
    extras = jnp.concatenate(
        [
            first_gain[:, None],
            second_gain[:, None],
            jnp.zeros((first_gain.shape[0], EXTRA - 2), LOW),
            router_weight,
            jnp.zeros((first_gain.shape[0], 128 - EXTRA - experts), LOW),
        ],
        axis=1,
    )
    bundle = jnp.concatenate(
        [extras, columns(query_weight), columns(key_weight), columns(value_weight)], axis=1
    )
    bucket_row = jnp.pad(bucket_ids, (0, 1))[None]
    padded_table = jnp.pad(bias_table, ((0, 16 - heads), (0, 0)))
    span = bucket_row.shape[1]
    weights = [bundle]
    if pairwise:
        weights += [swap(bundle, "fsdp", s) for s in range(2, owner_count, 2)]
        weights.append(swap(bundle, "fsdp", 1))
    far_tokens = swap(token_block, "seq", 2)
    near_tokens = swap(token_block, "seq", 1)
    (strip,) = call(
        strip_kernel, [padded_table, bucket_row], [((heads, STRIP, span), WIDE)], time=4
    )
    if pairwise:
        weights.append(swap(jnp.concatenate(weights[1:-1], axis=0), "fsdp", 1))
    else:
        weights = [lax.all_gather(bundle, "fsdp", axis=0, tiled=True)]
    token_parts = [token_block, near_tokens, far_tokens, swap(far_tokens, "seq", 1)]
    held, _, _ = lax.optimization_barrier((output_weight, weights, token_parts))
    output_weights = [lax.all_gather(held, "fsdp", axis=0, tiled=True)]

    kept, mixed_parts = forward_attention(where, token_parts, weights, strip, size)
    normed, q, k, v, wq, wk, wv, extra, o32, shares, attention = kept
    mixed_parts = exchange_seq(mixed_parts)

    hidden, normed_two, notes, both_slots = call(
        functools.partial(
            send_kernel,
            seq_count=seq_count,
            weight_parts=1,
            experts=experts,
            capacity=capacity,
        ),
        [*mixed_parts, *output_weights, token_block, grad_block, expert_ids[0], extra],
        [
            ((rows, features), WIDE),
            ((rows, features), LOW),
            ((rows, 128), WIDE),
            ((2 * slot_count, features), LOW),
        ],
        [pltpu.VMEM((features, features), LOW)],
        where,
        time=6,
    )
    received_both = exchange(both_slots).reshape(2 * slot_count, features)
    active, pre_grad, received, received_grad, back = expert_step(
        received_both, inner_weight[0], outer_weight[0], owner_count
    )
    returned = exchange(back).reshape(2 * slot_count, features)
    transposed = (((0,), (0,)), ((), ()))
    inner_term = product(received, pre_grad, transposed).astype(LOW)
    outer_term = product(active, received_grad, transposed).astype(LOW)
    inner_grad = lax.psum_scatter(inner_term, "seq", scatter_dimension=1, tiled=True)
    outer_grad = lax.psum_scatter(outer_term, "seq", scatter_dimension=0, tiled=True)

    results = call(
        functools.partial(
            return_kernel,
            seq_count=seq_count,
            weight_parts=1,
            experts=experts,
            capacity=capacity,
        ),
        [
            *mixed_parts,
            *output_weights,
            returned,
            hidden,
            normed_two,
            notes,
            grad_block,
            extra,
        ],
        [
            ((rows, features), LOW),
            ((rows, features), WIDE),
            ((features, features + 128), LOW),
        ]
        + [((rows, width), LOW)] * seq_count,
        [pltpu.VMEM((features, features), LOW)],
        where,
        time=8,
    )
    layer_out, hidden_grad, output_term = results[:3]
    mixed_grads = exchange_seq(results[3:])
    both = ("seq", "fsdp")
    device_count = seq_count * owner_count
    share = features // device_count
    held, _ = lax.optimization_barrier((output_term, mixed_grads))
    output_terms = lax.all_to_all(
        held.reshape(device_count, share, features + 128), both, 0, 0, tiled=True
    )
    dq, dkt, dvt, strip_grad = backward_attention(
        where, mixed_grads, q, k, v, o32, shares, attention, strip.shape
    )
    dq, output_terms = lax.optimization_barrier((dq, output_terms))
    (weight_terms,) = call(
        weight_kernel, [normed, dq, dkt, dvt], [((features, 3 * width), LOW)], time=6
    )
    held_dq, weight_terms = lax.optimization_barrier((dq, weight_terms))
    weight_terms = exchange(weight_terms)
    results = call(
        functools.partial(row_kernel, seq_count=seq_count),
        [normed, held_dq, dkt, dvt, wq, wk, wv, extra],
        [((rows, features), LOW)] * seq_count + [((1, features), WIDE)],
        [
            pltpu.VMEM((rows * seq_count, width), LOW),
            pltpu.VMEM((rows * seq_count, width), LOW),
        ],
        where,
        time=6,
    )
    row_grads, first_sum = results[:seq_count], results[seq_count]
    near, far = swap(row_grads[1], "seq", 1), swap(row_grads[3], "seq", 1)
    passed = (row_grads[2].astype(WIDE) + far.astype(WIDE)).astype(LOW)
    row_grads = [row_grads[0], near, swap(passed, "seq", 2)]
    (table_sums,) = call(
        functools.partial(table_kernel, bucket_count=bucket_count),
        [lax.optimization_barrier((strip_grad, first_sum))[0], bucket_row],
        [((8, bucket_count), WIDE)],
        time=5,
    )
    small = jnp.concatenate([first_sum.reshape(-1), table_sums[:heads].reshape(-1)])
    offset = 1
    while offset < owner_count:
        small = small + swap(small, "fsdp", offset)
        offset *= 2
    table_grad = small[features:].reshape(heads, bucket_count)
    small = small[:features]
    offset = 1
    while offset < seq_count:
        small = small + swap(small, "seq", offset)
        offset *= 2
    output_grad, others = call(
        sum_kernel, [output_terms], [((share, features), WIDE), ((share, 128), WIDE)]
    )
    (tokens_grad,) = call(
        functools.partial(finish_kernel, seq_count=len(row_grads)),
        [*row_grads, token_block, hidden_grad, extra],
        [((rows, features), LOW)],
        time=3,
    )
    first_grad = lax.dynamic_slice_in_dim(small, (me * owner_count + owner) * share, share, 0)
    weight_terms, inner_grad, outer_grad = lax.optimization_barrier(
        (weight_terms, inner_grad.astype(WIDE)[None], outer_grad.astype(WIDE)[None])
    )
    query_grad, key_grad, value_grad = call(
        sum_kernel, [weight_terms], [((features // owner_count, width), WIDE)] * 3
    )
    return (
        layer_out[None],
        tokens_grad[None],
        first_grad,
        query_grad,
        key_grad,
        value_grad,
        output_grad,
        table_grad,
        others[:, 1],
        others[:, EXTRA : EXTRA + experts],
        inner_grad,
        outer_grad,
    )


def solution(mesh):
    return jax.shard_map(
        on_device,
        mesh=mesh,
        in_specs=(
            P("fsdp", "seq", None),
            P("fsdp", "seq", None),
            P("fsdp", "seq", None),
            P(),
            P("fsdp"),
            P("fsdp", None),
            P("fsdp", None),
            P("fsdp", None),
            P("fsdp", None),
            P("seq", None),
            P("fsdp"),
            P("fsdp", None),
            P("fsdp", None, None),
            P("fsdp", None, None),
        ),
        out_specs=(
            P("fsdp", "seq", None),
            P("fsdp", "seq", None),
            P(("seq", "fsdp")),
            P("fsdp", "seq"),
            P("fsdp", "seq"),
            P("fsdp", "seq"),
            P(("seq", "fsdp"), None),
            P("seq", None),
            P(("seq", "fsdp")),
            P(("seq", "fsdp"), None),
            P("fsdp", None, "seq"),
            P("fsdp", "seq", None),
        ),
        check_vma=False,
    )
```

```python
import functools

import jax
import jax.numpy as jnp
from jax import lax
from jax.experimental import pallas as pl
from jax.experimental.pallas import tpu as pltpu
from jax.sharding import PartitionSpec as P

EPSILON = 1e-06
STRIP = 128
EXTRA = 8
VMEM_LIMIT = 56 * 1024 * 1024
NT = (((1,), (1,)), ((), ()))
NN = (((1,), (0,)), ((), ()))
LOW = jnp.bfloat16
WIDE = jnp.float32


def product(left, right, dims=NN):
    return lax.dot_general(left, right, dims, preferred_element_type=WIDE)


def flip(values):
    return values.astype(WIDE).T.astype(LOW)


def swap(values, axis, offset):
    count = lax.axis_size(axis)
    return lax.ppermute(values, axis, [(i, i ^ offset) for i in range(count)])


def cost(microseconds):
    return pl.CostEstimate(
        flops=int(microseconds * 1.15e9), bytes_accessed=1024, transcendentals=0
    )


def call(kernel, inputs, outputs, scratch=(), where=None, time=2):
    specs = [pl.BlockSpec(memory_space=pltpu.VMEM)] * len(inputs)
    operands = list(inputs)
    if where is not None:
        specs = [pl.BlockSpec(memory_space=pltpu.SMEM)] + specs
        operands = [where] + operands
    return pl.pallas_call(
        kernel,
        in_specs=specs,
        out_specs=[pl.BlockSpec(memory_space=pltpu.VMEM)] * len(outputs),
        out_shape=[jax.ShapeDtypeStruct(shape, dtype) for shape, dtype in outputs],
        scratch_shapes=list(scratch),
        compiler_params=pltpu.CompilerParams(vmem_limit_bytes=VMEM_LIMIT),
        cost_estimate=cost(time),
    )(*operands)


def strip_kernel(table_ref, bucket_ref, strip_ref):
    heads = strip_ref.shape[0]
    span = bucket_ref.shape[1]
    ids = lax.broadcasted_iota(jnp.int32, (table_ref.shape[1], span), 0)
    hot = jnp.where(ids == bucket_ref[...], 1.0, 0.0).astype(LOW)
    relative = product(table_ref[...], hot)
    for head in range(heads):
        wide = jnp.broadcast_to(relative[head : head + 1, :], (STRIP, span))
        strip_ref[head] = pltpu.roll(wide, span - STRIP + 1, 1, stride=1, stride_axis=0)


def forward_kernel(where_ref, *refs, heads, size, seq_count, weight_parts):
    token_refs = refs[:seq_count]
    weight_refs = refs[seq_count : seq_count + weight_parts]
    strip_ref = refs[seq_count + weight_parts]
    (
        normed_ref, q_ref, k_ref, v_ref, wq_ref, wk_ref, wv_ref, extra_ref, o32_ref, share_ref,
        weights_ref,
    ) = refs[seq_count + weight_parts + 1 : seq_count + weight_parts + 12]
    mixed_refs = refs[seq_count + weight_parts + 12 : -2]
    joined_ref, vext_ref = refs[-2:]
    length, width = k_ref.shape
    rows = length // seq_count
    step = pl.program_id(0)
    me = where_ref[0]
    owner_row = where_ref[1]

    @pl.when(step == 0)
    def _():
        if weight_parts == 1:
            joined_ref[...] = weight_refs[0][...]
        else:
            share = weight_refs[0].shape[0]
            offsets = [2 * part for part in range(weight_parts - 2)] + [1]
            for part, offset in enumerate(offsets):
                place = pl.multiple_of((owner_row ^ offset) * share, 16)
                joined_ref[pl.ds(place, share), :] = weight_refs[part][...]
            for part in range(1, weight_parts - 2):
                place = pl.multiple_of((owner_row ^ (2 * part + 1)) * share, 16)
                joined_ref[pl.ds(place, share), :] = weight_refs[-1][
                    (part - 1) * share : part * share, :
                ]
        extra_ref[...] = joined_ref[:, :128].astype(WIDE).T
        joined = joined_ref[...]
        wq_ref[...] = joined[:, 128 : 128 + width]
        wk_ref[...] = joined[:, 128 + width : 128 + 2 * width]
        wv_ref[...] = joined[:, 128 + 2 * width : 128 + 3 * width]
        gain = extra_ref[0:1, :]
        for part in range(seq_count):
            place = pl.ds(pl.multiple_of((me ^ part) * rows, rows), rows)
            inputs = token_refs[part][...].astype(WIDE)
            factor = lax.rsqrt(jnp.mean(inputs * inputs, axis=1, keepdims=True) + EPSILON)
            normed = (inputs * factor * gain).astype(LOW)
            normed_ref[place, :] = normed
            q_ref[place, :] = product(normed, wq_ref[...]).astype(LOW)
            k_ref[place, :] = product(normed, wk_ref[...]).astype(LOW)
            values = product(normed, wv_ref[...]).astype(LOW)
            v_ref[place, :] = values
            vext_ref[place, :width] = values
        vext_ref[:, width:] = jnp.ones((length, 256 - width), LOW)

    for part in range(rows // STRIP):
        block = (me ^ step) * (rows // STRIP) + part
        start = pl.multiple_of((length // STRIP - 1 - block) * STRIP, STRIP)
        q = q_ref[pl.ds(pl.multiple_of(block * STRIP, STRIP), STRIP), :]
        owner = lax.broadcasted_iota(jnp.int32, (STRIP, width), 1) // size
        lanes = lax.broadcasted_iota(jnp.int32, (STRIP, 128), 1)
        total = jnp.zeros((STRIP, width), WIDE)
        shares = jnp.zeros((STRIP, 128), WIDE)
        place = slice(part * STRIP, (part + 1) * STRIP)
        for head in range(heads):
            scores = product(jnp.where(owner == head, q, jnp.zeros_like(q)), k_ref[...], NT)
            scores = scores + strip_ref[head, :, pl.ds(start, length)]
            high = jnp.max(scores, axis=1, keepdims=True)
            weights = jnp.exp(scores - high).astype(LOW)
            mixed = product(weights, vext_ref[...])
            weights_ref[head, place, :] = weights
            share = 1.0 / mixed[:, width : width + 1]
            total = jnp.where(owner == head, mixed[:, :width] * share, total)
            shares = jnp.where(lanes == head, share, shares)
        o32_ref[place, :] = total
        share_ref[place, :] = shares
        for offset in range(seq_count):

            @pl.when(step == offset)
            def _():
                mixed_refs[offset][place, :] = total.astype(LOW)


def forward_attention(where, token_parts, weight_parts, strip, size):
    seq_count = len(token_parts)
    rows, features = token_parts[0].shape
    length = rows * seq_count
    columns = weight_parts[0].shape[1]
    width = (columns - 128) // 3
    heads = width // size
    full = lambda *shape: pl.BlockSpec(shape, lambda i, w: (0,) * len(shape))
    block = lambda w: pl.BlockSpec((rows, w), lambda i, w_: (i, 0))
    shaped = jax.ShapeDtypeStruct
    results = pl.pallas_call(
        functools.partial(
            forward_kernel,
            heads=heads,
            size=size,
            seq_count=seq_count,
            weight_parts=len(weight_parts),
        ),
        grid_spec=pltpu.PrefetchScalarGridSpec(
            num_scalar_prefetch=1,
            grid=(seq_count,),
            in_specs=[full(*a.shape) for a in (*token_parts, *weight_parts, strip)],
            out_specs=[full(length, features)]
            + [full(length, width)] * 3
            + [full(features, width)] * 3
            + [full(128, features), block(width), block(128)]
            + [pl.BlockSpec((heads, rows, length), lambda i, w: (0, i, 0))]
            + [full(rows, width)] * seq_count,
            scratch_shapes=[pltpu.VMEM((features, columns), LOW), pltpu.VMEM((length, 256), LOW)],
        ),
        out_shape=[shaped((length, features), LOW)]
        + [shaped((length, width), LOW)] * 3
        + [shaped((features, width), LOW)] * 3
        + [
            shaped((128, features), WIDE),
            shaped((length, width), WIDE),
            shaped((length, 128), WIDE),
            shaped((heads, length, length), LOW),
        ]
        + [shaped((rows, width), LOW)] * seq_count,
        compiler_params=pltpu.CompilerParams(vmem_limit_bytes=VMEM_LIMIT),
        cost_estimate=cost(35),
    )(where, *token_parts, *weight_parts, strip)
    return results[:11], results[11:]


def place_rows(where_ref, joined_ref, part_refs):
    part_rows = joined_ref.shape[0] // len(part_refs)
    for part, part_ref in enumerate(part_refs):
        place = pl.multiple_of((where_ref[1] ^ part) * part_rows, 16) if len(part_refs) > 1 else 0
        joined_ref[pl.ds(place, part_rows), :] = part_ref[...]


def send_kernel(where_ref, *refs, seq_count, weight_parts, experts, capacity):
    mixed_refs = refs[:seq_count]
    weight_refs = refs[seq_count : seq_count + weight_parts]
    tokens_ref, cotangent_ref, ids_ref, extra_ref = refs[
        seq_count + weight_parts : seq_count + weight_parts + 4
    ]
    rest = refs[seq_count + weight_parts + 4 :]
    hidden_ref, normed_ref, notes_ref = rest[:3]
    both_ref, joined_ref = rest[3:]
    rows = tokens_ref.shape[0]
    width = mixed_refs[0].shape[1]
    place_rows(where_ref, joined_ref, weight_refs)
    hidden = tokens_ref[...].astype(WIDE)
    for part in range(seq_count):
        place = pl.multiple_of((where_ref[0] ^ part) * width, 64)
        hidden = hidden + product(mixed_refs[part][...], joined_ref[pl.ds(place, width), :])
    hidden_ref[...] = hidden
    factor = lax.rsqrt(jnp.mean(hidden * hidden, axis=1, keepdims=True) + EPSILON)
    normed = (hidden * factor * extra_ref[1:2, :]).astype(LOW)
    normed_ref[...] = normed
    logits = product(normed, extra_ref[...].astype(LOW), NT)
    lanes = lax.broadcasted_iota(jnp.int32, (rows, 128), 1)
    valid = (lanes >= EXTRA) & (lanes < EXTRA + experts)
    logits = jnp.where(valid, logits, -jnp.inf)
    powers = jnp.exp(logits - jnp.max(logits, axis=1, keepdims=True))
    probs = powers / jnp.sum(powers, axis=1, keepdims=True)
    ids = ids_ref[...]
    hot = lanes == ids + EXTRA
    gate = jnp.sum(jnp.where(hot, probs, 0.0), axis=1, keepdims=True)
    earlier_rows = lax.broadcasted_iota(jnp.int32, (rows, rows), 1) < lax.broadcasted_iota(
        jnp.int32, (rows, rows), 0
    )
    earlier = product(
        jnp.where(earlier_rows, 1.0, 0.0).astype(LOW), jnp.where(hot, 1.0, 0.0).astype(LOW)
    )
    slot = jnp.sum(jnp.where(hot, earlier, 0.0), axis=1, keepdims=True)
    placement = (ids * (2 * capacity)).astype(WIDE) + slot
    notes = jnp.where(lanes == 0, gate, probs)
    notes = jnp.where(lanes == 1, placement, notes)
    notes = jnp.where(lanes == 2, factor, notes)
    notes = jnp.where(lanes == 3, (ids + EXTRA).astype(WIDE), notes)
    notes_ref[...] = notes
    placement_row = notes.T[1:2, :].astype(jnp.int32)
    slot_ids = lax.broadcasted_iota(jnp.int32, (2 * experts * capacity, rows), 0)
    spread = jnp.concatenate(
        [
            jnp.where(slot_ids == placement_row, 1.0, 0.0).astype(LOW),
            jnp.where(slot_ids == placement_row + capacity, 1.0, 0.0).astype(LOW),
        ],
        axis=1,
    )
    picked_grad = (gate * cotangent_ref[...].astype(WIDE)).astype(LOW)
    both_ref[...] = product(spread, jnp.concatenate([normed, picked_grad], axis=0)).astype(LOW)


def expert_kernel(
    both_ref, inner_ref, outer_ref, active_ref, pre_grad_ref, slots_ref, grads_ref, back_ref,
    out_ref, slots_grad_ref, *, sources,
):
    step = pl.program_id(0)
    slot_count, features = slots_ref.shape
    apart = (sources, 2, slot_count // sources, features)

    @pl.when(step == 0)
    def _():
        both = both_ref[...].astype(WIDE).reshape(apart)
        slots_ref[...] = both[:, 0].reshape(slot_count, features).astype(LOW)
        grads_ref[...] = both[:, 1].reshape(slot_count, features).astype(LOW)
        out_ref[...] = jnp.zeros_like(out_ref)
        slots_grad_ref[...] = jnp.zeros_like(slots_grad_ref)

    pre = product(slots_ref[...], inner_ref[...])
    active_grad = product(grads_ref[...], outer_ref[...], NT)
    scale = 0.7978845608028654
    square = pre * pre
    bent = jnp.tanh(pre * (scale + scale * 0.044715 * square))
    half = 0.5 + 0.5 * bent
    active = (pre * half).astype(LOW)
    slope = half + 0.5 * pre * (1.0 - bent * bent) * (scale + 3.0 * scale * 0.044715 * square)
    pre_grad = (active_grad * slope).astype(LOW)
    active_ref[...] = active
    pre_grad_ref[...] = pre_grad
    out_ref[...] += product(active, outer_ref[...])
    slots_grad_ref[...] += product(pre_grad, inner_ref[...], NT)

    @pl.when(step == pl.num_programs(0) - 1)
    def _():
        each = (sources, 1, slot_count // sources, features)
        back = jnp.concatenate(
            [out_ref[...].reshape(each), slots_grad_ref[...].reshape(each)], axis=1
        )
        back_ref[...] = back.reshape(2 * slot_count, features).astype(LOW)


def expert_step(both, inner, outer, sources, chunk=512):
    slot_count = both.shape[0] // 2
    features, units = inner.shape
    full = lambda *shape: pl.BlockSpec(shape, lambda i: (0,) * len(shape))
    across = pl.BlockSpec((slot_count, chunk), lambda i: (0, i))
    shaped = jax.ShapeDtypeStruct
    return pl.pallas_call(
        functools.partial(expert_kernel, sources=sources),
        grid=(units // chunk,),
        in_specs=[
            full(2 * slot_count, features),
            pl.BlockSpec((features, chunk), lambda i: (0, i)),
            pl.BlockSpec((chunk, features), lambda i: (i, 0)),
        ],
        out_specs=[
            across,
            across,
            full(slot_count, features),
            full(slot_count, features),
            full(2 * slot_count, features),
        ],
        out_shape=[
            shaped((slot_count, units), LOW),
            shaped((slot_count, units), LOW),
            shaped((slot_count, features), LOW),
            shaped((slot_count, features), LOW),
            shaped((2 * slot_count, features), LOW),
        ],
        scratch_shapes=[
            pltpu.VMEM((slot_count, features), WIDE),
            pltpu.VMEM((slot_count, features), WIDE),
        ],
        compiler_params=pltpu.CompilerParams(vmem_limit_bytes=VMEM_LIMIT),
        cost_estimate=cost(24),
    )(both, inner, outer)


def return_kernel(where_ref, *refs, seq_count, weight_parts, experts, capacity):
    mixed_refs = refs[:seq_count]
    weight_refs = refs[seq_count : seq_count + weight_parts]
    refs = refs[seq_count + weight_parts :]
    back_ref = refs[0]
    refs = refs[1:]
    hidden_ref, normed_ref, notes_ref, cotangent_ref, extra_ref = refs[:5]
    layer_ref, hidden_grad_ref, output_grad_ref = refs[5:8]
    mixed_grad_refs = refs[8 : 8 + seq_count]
    joined_ref = refs[-1]
    rows, features = hidden_ref.shape
    width = mixed_refs[0].shape[1]
    place_rows(where_ref, joined_ref, weight_refs)
    notes = notes_ref[...]
    gate = notes[:, 0:1]
    placement = notes[:, 1:2].astype(jnp.int32)
    factor = notes[:, 2:3]
    own_lane = notes[:, 3:4].astype(jnp.int32)
    hidden = hidden_ref[...]
    cotangent = cotangent_ref[...].astype(WIDE)
    slot_ids = lax.broadcasted_iota(jnp.int32, (rows, back_ref.shape[0]), 1)
    picked = product(jnp.where(slot_ids == placement, 1.0, 0.0).astype(LOW), back_ref[...])
    layer_ref[...] = (hidden + gate * picked).astype(LOW)
    gate_grad = jnp.sum(cotangent * picked, axis=1, keepdims=True)
    lanes = lax.broadcasted_iota(jnp.int32, (rows, 128), 1)
    valid = (lanes >= EXTRA) & (lanes < EXTRA + experts)
    probs = jnp.where(valid, notes, 0.0)
    prob_grad = jnp.where(lanes == own_lane, gate_grad, 0.0)
    logit_grad = probs * (prob_grad - gate * gate_grad)
    logit_grad_low = logit_grad.astype(LOW)
    normed_grad = product(
        jnp.where(slot_ids == placement + capacity, 1.0, 0.0).astype(LOW), back_ref[...]
    )
    normed_grad = normed_grad + product(logit_grad_low, extra_ref[...].astype(LOW))
    scaled = normed_grad * hidden
    gain = extra_ref[1:2, :]
    center = jnp.mean(scaled * gain, axis=1, keepdims=True)
    hidden_grad = cotangent + factor * (gain * normed_grad) - hidden * (
        factor * factor * factor * center
    )
    hidden_grad_ref[...] = hidden_grad
    small = product(logit_grad.T.astype(LOW), normed_ref[...])
    gain_grad = jnp.sum(scaled * factor, axis=0, keepdims=True)
    small = jnp.where(lax.broadcasted_iota(jnp.int32, small.shape, 0) == 1, gain_grad, small)
    output_grad_ref[:, features:] = small.T.astype(LOW)
    branch = hidden_grad.astype(LOW)
    for part in range(seq_count):
        place = pl.ds(pl.multiple_of((where_ref[0] ^ part) * width, 64), width)
        mixed_grad_refs[part][...] = product(branch, joined_ref[place, :], NT).astype(LOW)
        output_grad_ref[place, :features] = product(flip(mixed_refs[part][...]), branch).astype(
            LOW
        )


def three_parts(value):
    first = value.astype(LOW)
    rest = value - first.astype(WIDE)
    second = rest.astype(LOW)
    third = (rest - second.astype(WIDE)).astype(LOW)
    return first, second, third


def attend_back_kernel(where_ref, *refs, heads, size, seq_count):
    grad_refs = refs[:seq_count]
    q_ref, k_ref, v_ref, o32_ref, share_ref, weights_ref = refs[seq_count : seq_count + 6]
    dq_ref, dkt_ref, dvt_ref, strip_grad_ref = refs[seq_count + 6 : seq_count + 10]
    vext_ref, grad_ref = refs[seq_count + 10 :]
    length, width = k_ref.shape
    rows = length // seq_count
    step = pl.program_id(0)
    me = where_ref[0]

    @pl.when(step == 0)
    def _():
        vext_ref[:, :width] = v_ref[...]
        vext_ref[:, width:] = jnp.ones((length, 256 - width), LOW)
        dkt_ref[...] = jnp.zeros_like(dkt_ref)
        dvt_ref[...] = jnp.zeros_like(dvt_ref)
        strip_grad_ref[...] = jnp.zeros_like(strip_grad_ref)

    for offset in range(seq_count):

        @pl.when(step == offset)
        def _():
            grad_ref[...] = grad_refs[offset][...]

    for part in range(rows // STRIP):
        block = (me ^ step) * (rows // STRIP) + part
        start = pl.multiple_of((length // STRIP - 1 - block) * STRIP, STRIP)
        token_rows = pl.ds(pl.multiple_of(block * STRIP, STRIP), STRIP)
        own_rows = slice(part * STRIP, (part + 1) * STRIP)
        owner = lax.broadcasted_iota(jnp.int32, (STRIP, width), 1) // size
        tail = lax.broadcasted_iota(jnp.int32, (STRIP, 256 - width), 1)
        share = jnp.zeros((STRIP, width), WIDE)
        for head in range(heads):
            share = jnp.where(owner == head, share_ref[own_rows, head : head + 1], share)
        scaled = grad_ref[own_rows, :].astype(WIDE) * share
        mixed_product = scaled * o32_ref[own_rows, :]
        grad_flipped = scaled.T.astype(LOW)
        scaled = scaled.astype(LOW)
        q_flipped = flip(q_ref[token_rows, :])
        total = jnp.zeros((STRIP, width), WIDE)
        for head in range(heads):
            mine = owner == head
            head_rows = slice(head * size, (head + 1) * size)
            delta = jnp.sum(jnp.where(mine, mixed_product, 0.0), axis=1, keepdims=True)
            first, second, third = three_parts(-delta)
            added = jnp.where(tail == 2, third, jnp.zeros_like(third))
            added = jnp.where(tail == 0, first, jnp.where(tail == 1, second, added))
            own_grad = jnp.concatenate([jnp.where(mine, scaled, jnp.zeros_like(scaled)), added], 1)
            weights = weights_ref[head, own_rows, :]
            score_grad = weights.astype(WIDE) * product(own_grad, vext_ref[...], NT)
            strip_grad_ref[head, :, pl.ds(start, length)] += score_grad
            score_grad = score_grad.astype(LOW)
            dvt_ref[head_rows, :] += product(grad_flipped[head_rows, :], weights)
            dkt_ref[head_rows, :] += product(q_flipped[head_rows, :], score_grad)
            total = jnp.where(mine, product(score_grad, k_ref[...]), total)
        dq_ref[token_rows, :] = total.astype(LOW)


def backward_attention(where, grad_parts, q, k, v, o32, shares, attention, strip_shape):
    seq_count = len(grad_parts)
    length, width = q.shape
    rows = length // seq_count
    heads = attention.shape[0]
    full = lambda *shape: pl.BlockSpec(shape, lambda i, w: (0,) * len(shape))
    block = lambda w: pl.BlockSpec((rows, w), lambda i, w_: (i, 0))
    shaped = jax.ShapeDtypeStruct
    return pl.pallas_call(
        functools.partial(
            attend_back_kernel, heads=heads, size=width // heads, seq_count=seq_count
        ),
        grid_spec=pltpu.PrefetchScalarGridSpec(
            num_scalar_prefetch=1,
            grid=(seq_count,),
            in_specs=[full(rows, width)] * seq_count
            + [full(length, width)] * 3
            + [block(width), block(128)]
            + [pl.BlockSpec((heads, rows, length), lambda i, w: (0, i, 0))],
            out_specs=[
                full(length, width),
                full(width, length),
                full(width, length),
                full(*strip_shape),
            ],
            scratch_shapes=[pltpu.VMEM((length, 256), LOW), pltpu.VMEM((rows, width), LOW)],
        ),
        out_shape=[
            shaped((length, width), LOW),
            shaped((width, length), WIDE),
            shaped((width, length), WIDE),
            shaped(strip_shape, WIDE),
        ],
        compiler_params=pltpu.CompilerParams(vmem_limit_bytes=VMEM_LIMIT),
        cost_estimate=cost(32),
    )(where, *grad_parts, q, k, v, o32, shares, attention)


def weight_kernel(normed_ref, dq_ref, dkt_ref, dvt_ref, out_ref):
    flipped = jnp.concatenate(
        [flip(dq_ref[...]), dkt_ref[...].astype(LOW), dvt_ref[...].astype(LOW)], axis=0
    )
    out_ref[...] = product(flipped, normed_ref[...]).T.astype(LOW)


def row_kernel(
    where_ref, normed_ref, dq_ref, dkt_ref, dvt_ref, wq_ref, wk_ref, wv_ref, extra_ref, *refs,
    seq_count,
):
    row_refs = refs[:seq_count]
    gain_ref, dk_ref, dv_ref = refs[seq_count:]
    length, width = dq_ref.shape
    rows = length // seq_count
    dk_ref[...] = dkt_ref[...].T.astype(LOW)
    dv_ref[...] = dvt_ref[...].T.astype(LOW)
    gain_sum = jnp.zeros((1, normed_ref.shape[1]), WIDE)
    for part in range(seq_count):
        place = pl.ds(pl.multiple_of((where_ref[0] ^ part) * rows, rows), rows)
        row_grad = product(dq_ref[place, :], wq_ref[...], NT)
        row_grad = row_grad + product(dk_ref[place, :], wk_ref[...], NT)
        row_grad = row_grad + product(dv_ref[place, :], wv_ref[...], NT)
        row_refs[part][...] = row_grad.astype(LOW)
        gain_sum = gain_sum + jnp.sum(
            row_grad * normed_ref[place, :].astype(WIDE), axis=0, keepdims=True
        )
    gain_ref[...] = gain_sum / extra_ref[0:1, :]


def table_kernel(strip_grad_ref, bucket_ref, out_ref, *, bucket_count):
    heads, _, span = strip_grad_ref.shape
    sums = []
    for head in range(heads):
        folded = strip_grad_ref[head]
        half = STRIP // 2
        while half >= 1:
            folded = pltpu.roll(folded[:half], half, 1) + folded[half:]
            half //= 2
        sums.append(folded)
    diagonals = jnp.concatenate(sums + [jnp.zeros((8 - heads, span), WIDE)], axis=0)
    ids = lax.broadcasted_iota(jnp.int32, (bucket_count, span), 0)
    hot = jnp.where(ids == bucket_ref[...], 1.0, 0.0)
    out_ref[...] = lax.dot_general(
        diagonals, hot, NT, preferred_element_type=WIDE, precision=lax.Precision.HIGHEST
    )


def finish_kernel(*refs, seq_count):
    row_refs = refs[:seq_count]
    tokens_ref, hidden_grad_ref, extra_ref, out_ref = refs[seq_count:]
    normed_grad = row_refs[0][...].astype(WIDE)
    for part in range(1, seq_count):
        normed_grad = normed_grad + row_refs[part][...].astype(WIDE)
    inputs = tokens_ref[...].astype(WIDE)
    factor = lax.rsqrt(jnp.mean(inputs * inputs, axis=1, keepdims=True) + EPSILON)
    scaled = normed_grad * extra_ref[0:1, :]
    center = jnp.mean(scaled * inputs, axis=1, keepdims=True)
    out_ref[...] = (
        hidden_grad_ref[...] + factor * scaled - inputs * (factor * factor * factor * center)
    ).astype(LOW)


def sum_kernel(parts_ref, *out_refs):
    total = parts_ref[0].astype(WIDE)
    for part in range(1, parts_ref.shape[0]):
        total = total + parts_ref[part].astype(WIDE)
    start = 0
    for out_ref in out_refs:
        width = out_ref.shape[1]
        out_ref[...] = total[:, start : start + width]
        start += width


def on_device(
    tokens,
    cotangent,
    expert_ids,
    bucket_ids,
    first_gain,
    query_weight,
    key_weight,
    value_weight,
    output_weight,
    bias_table,
    second_gain,
    router_weight,
    inner_weight,
    outer_weight,
):
    seq_count = lax.axis_size("seq")
    owner_count = lax.axis_size("fsdp")
    pairwise = owner_count <= 8
    me = lax.axis_index("seq").astype(jnp.int32)
    owner = lax.axis_index("fsdp").astype(jnp.int32)
    rows, features = tokens.shape[1:]
    experts = router_weight.shape[1]
    capacity = max(2, 4 * rows // (3 * experts))
    slot_count = experts * capacity
    heads, bucket_count = bias_table.shape
    width = features // seq_count
    size = width // heads
    where = jnp.stack([me, owner, jnp.zeros_like(owner)])
    weight_parts = owner_count if pairwise else 1

    def exchange(values):
        split = values.reshape(owner_count, -1, values.shape[1])
        return lax.all_to_all(split, "fsdp", 0, 0, tiled=True)

    def exchange_seq(parts):
        return [parts[0]] + [swap(parts[s], "seq", s) for s in range(1, seq_count)]

    token_block = tokens[0]
    grad_block = cotangent[0]
    columns = lambda weight: lax.dynamic_slice_in_dim(weight, me * width, width, 1)
    extras = jnp.concatenate(
        [
            first_gain[:, None],
            second_gain[:, None],
            jnp.zeros((first_gain.shape[0], EXTRA - 2), LOW),
            router_weight,
            jnp.zeros((first_gain.shape[0], 128 - EXTRA - experts), LOW),
        ],
        axis=1,
    )
    bundle = jnp.concatenate(
        [extras, columns(query_weight), columns(key_weight), columns(value_weight)], axis=1
    )
    bucket_row = jnp.pad(bucket_ids, (0, 1))[None]
    padded_table = jnp.pad(bias_table, ((0, 16 - heads), (0, 0)))
    span = bucket_row.shape[1]
    weights = [bundle]
    if pairwise:
        weights += [swap(bundle, "fsdp", s) for s in range(2, owner_count, 2)]
        weights.append(swap(bundle, "fsdp", 1))
    far_tokens = swap(token_block, "seq", 2)
    near_tokens = swap(token_block, "seq", 1)
    (strip,) = call(
        strip_kernel, [padded_table, bucket_row], [((heads, STRIP, span), WIDE)], time=4
    )
    if pairwise:
        weights.append(swap(jnp.concatenate(weights[1:-1], axis=0), "fsdp", 1))
    else:
        weights = [lax.all_gather(bundle, "fsdp", axis=0, tiled=True)]
    token_parts = [token_block, near_tokens, far_tokens, swap(far_tokens, "seq", 1)]
    held, _, _ = lax.optimization_barrier((output_weight, weights, token_parts))
    output_weights = [lax.all_gather(held, "fsdp", axis=0, tiled=True)]

    kept, mixed_parts = forward_attention(where, token_parts, weights, strip, size)
    normed, q, k, v, wq, wk, wv, extra, o32, shares, attention = kept
    mixed_parts = exchange_seq(mixed_parts)

    hidden, normed_two, notes, both_slots = call(
        functools.partial(
            send_kernel,
            seq_count=seq_count,
            weight_parts=1,
            experts=experts,
            capacity=capacity,
        ),
        [*mixed_parts, *output_weights, token_block, grad_block, expert_ids[0], extra],
        [
            ((rows, features), WIDE),
            ((rows, features), LOW),
            ((rows, 128), WIDE),
            ((2 * slot_count, features), LOW),
        ],
        [pltpu.VMEM((features, features), LOW)],
        where,
        time=6,
    )
    received_both = exchange(both_slots).reshape(2 * slot_count, features)
    active, pre_grad, received, received_grad, back = expert_step(
        received_both, inner_weight[0], outer_weight[0], owner_count
    )
    returned = exchange(back).reshape(2 * slot_count, features)
    transposed = (((0,), (0,)), ((), ()))
    inner_term = product(received, pre_grad, transposed).astype(LOW)
    outer_term = product(active, received_grad, transposed).astype(LOW)
    inner_grad = lax.psum_scatter(inner_term, "seq", scatter_dimension=1, tiled=True)
    outer_grad = lax.psum_scatter(outer_term, "seq", scatter_dimension=0, tiled=True)

    results = call(
        functools.partial(
            return_kernel,
            seq_count=seq_count,
            weight_parts=1,
            experts=experts,
            capacity=capacity,
        ),
        [
            *mixed_parts,
            *output_weights,
            returned,
            hidden,
            normed_two,
            notes,
            grad_block,
            extra,
        ],
        [
            ((rows, features), LOW),
            ((rows, features), WIDE),
            ((features, features + 128), LOW),
        ]
        + [((rows, width), LOW)] * seq_count,
        [pltpu.VMEM((features, features), LOW)],
        where,
        time=8,
    )
    layer_out, hidden_grad, output_term = results[:3]
    mixed_grads = exchange_seq(results[3:])
    both = ("seq", "fsdp")
    device_count = seq_count * owner_count
    share = features // device_count
    held, _ = lax.optimization_barrier((output_term, mixed_grads))
    output_terms = lax.all_to_all(
        held.reshape(device_count, share, features + 128), both, 0, 0, tiled=True
    )
    dq, dkt, dvt, strip_grad = backward_attention(
        where, mixed_grads, q, k, v, o32, shares, attention, strip.shape
    )
    (weight_terms,) = call(
        weight_kernel, [normed, dq, dkt, dvt], [((features, 3 * width), LOW)], time=6
    )
    held_dq, weight_terms, output_terms = lax.optimization_barrier(
        (dq, weight_terms, output_terms)
    )
    weight_terms = exchange(weight_terms)
    results = call(
        functools.partial(row_kernel, seq_count=seq_count),
        [normed, held_dq, dkt, dvt, wq, wk, wv, extra],
        [((rows, features), LOW)] * seq_count + [((1, features), WIDE)],
        [
            pltpu.VMEM((rows * seq_count, width), LOW),
            pltpu.VMEM((rows * seq_count, width), LOW),
        ],
        where,
        time=6,
    )
    row_grads, first_sum = results[:seq_count], results[seq_count]
    near, far = swap(row_grads[1], "seq", 1), swap(row_grads[3], "seq", 1)
    passed = (row_grads[2].astype(WIDE) + far.astype(WIDE)).astype(LOW)
    row_grads = [row_grads[0], near, swap(passed, "seq", 2)]
    (table_sums,) = call(
        functools.partial(table_kernel, bucket_count=bucket_count),
        [lax.optimization_barrier((strip_grad, first_sum))[0], bucket_row],
        [((8, bucket_count), WIDE)],
        time=5,
    )
    small = jnp.concatenate([first_sum.reshape(-1), table_sums[:heads].reshape(-1)])
    offset = 1
    while offset < owner_count:
        small = small + swap(small, "fsdp", offset)
        offset *= 2
    table_grad = small[features:].reshape(heads, bucket_count)
    small = small[:features]
    offset = 1
    while offset < seq_count:
        small = small + swap(small, "seq", offset)
        offset *= 2
    output_grad, others = call(
        sum_kernel, [output_terms], [((share, features), WIDE), ((share, 128), WIDE)]
    )
    (tokens_grad,) = call(
        functools.partial(finish_kernel, seq_count=len(row_grads)),
        [*row_grads, token_block, hidden_grad, extra],
        [((rows, features), LOW)],
        time=3,
    )
    first_grad = lax.dynamic_slice_in_dim(small, (me * owner_count + owner) * share, share, 0)
    weight_terms, inner_grad, outer_grad = lax.optimization_barrier(
        (weight_terms, inner_grad.astype(WIDE)[None], outer_grad.astype(WIDE)[None])
    )
    query_grad, key_grad, value_grad = call(
        sum_kernel, [weight_terms], [((features // owner_count, width), WIDE)] * 3
    )
    return (
        layer_out[None],
        tokens_grad[None],
        first_grad,
        query_grad,
        key_grad,
        value_grad,
        output_grad,
        table_grad,
        others[:, 1],
        others[:, EXTRA : EXTRA + experts],
        inner_grad,
        outer_grad,
    )


def solution(mesh):
    return jax.shard_map(
        on_device,
        mesh=mesh,
        in_specs=(
            P("fsdp", "seq", None),
            P("fsdp", "seq", None),
            P("fsdp", "seq", None),
            P(),
            P("fsdp"),
            P("fsdp", None),
            P("fsdp", None),
            P("fsdp", None),
            P("fsdp", None),
            P("seq", None),
            P("fsdp"),
            P("fsdp", None),
            P("fsdp", None, None),
            P("fsdp", None, None),
        ),
        out_specs=(
            P("fsdp", "seq", None),
            P("fsdp", "seq", None),
            P(("seq", "fsdp")),
            P("fsdp", "seq"),
            P("fsdp", "seq"),
            P("fsdp", "seq"),
            P(("seq", "fsdp"), None),
            P("seq", None),
            P(("seq", "fsdp")),
            P(("seq", "fsdp"), None),
            P("fsdp", None, "seq"),
            P("fsdp", "seq", None),
        ),
        check_vma=False,
    )
```
